512 devices in a mesh: rep: 32 (over y_hi, x, core), grp: 16 (over z, y_lo).
Axes of the slice: x: 4, y: 8 (y_hi: 4, y_lo: 2; y = y_hi * 2 + y_lo), z: 8, core: 2. Of those that a mesh axis runs over, the one named last changes fastest.
Arguments:
- q_nope: bfloat16 [1024, 2, 128, 128], P('rep', None, 'grp'), may hold values from -6 to 6
- q_rope: bfloat16 [1024, 2, 128, 64], P('rep', None, 'grp'), may hold values from -48 to 48
- new_latent: bfloat16 [1024, 2, 576], P('rep'), may hold values from -6 to 6
- w_uk: bfloat16 [128, 128, 512], P('grp'), may hold values from -0.5 to 0.5
- w_uv: bfloat16 [128, 512, 128], P('grp'), may hold values from -3 to 3
- prefix_store: bfloat16 [32, 2048, 576], P('rep', 'grp'), may hold values from -6 to 6
- store_order: int32 [32], replicated, may hold values from 0 to 31, each once
- prefix_of_group: int32 [32], replicated, may hold values from 0 to 3
- private_store: bfloat16 [32, 32, 2, 256, 576], P('rep', None, None, 'grp'), may hold values from -6 to 6
- request_source: int32 [1024, 1], P('rep'), may hold values from 0 to 31; in each aligned block of 32 rows (0 to 31, 32 to 63, ...) at most 2 rows name the same one
- private_len: int32 [32, 32], P('rep'), may hold values from 1 to 256, 6144 in all within a row
Outputs:
- head_values: bfloat16 [1024, 2, 128, 128], P('rep', None, 'grp')
The draws below stay inside these ranges and needn't reach their ends.
Inputs may be any that keep to these rules, and one draw needn't show every extreme that they name: `request_source`: within the 32 rows of one decode group no source is named more than 2 times.
All inputs are finite; a program needn't handle non-finite values.
Results may differ from the reference program's by a relative error of at most 0.02.
Values may be sent and summed in bfloat16 or wider, within the bound.
A program may use at most 64 MiB of HBM per device.

```python
import math
import jax
import jax.numpy as jnp
import numpy as np
from jax import lax

H = 128
DC = 512
DR = 64
DN = 128
DV = 128
REQ = 32
STEPS = 2
PLEN = 2048
PRIV = 256
NPREF = 4
GROUPS = 32
ROWS = 1024
CAP = 2


def draw_q_rope(key, part):
    key = jax.random.fold_in(key, 3)
    values = jnp.clip(jax.random.normal(key, (ROWS, STEPS, H, DR), jnp.float32), -6.0, 6.0)
    return values.astype(jnp.bfloat16)


def draw_new_latent(key, part):
    key = jax.random.fold_in(key, 5)
    values = jnp.clip(jax.random.normal(key, (ROWS, STEPS, DC + DR), jnp.float32), -6.0, 6.0)
    return values.astype(jnp.bfloat16)


def touch_ends(array, rng, low, largest):
    place = [jax.random.randint(jax.random.fold_in(rng, axis), (), 0, length) for axis, length in enumerate(array.shape)]
    main_axis = array.shape.index(max(array.shape))
    neighbour = place[:main_axis] + [(place[main_axis] + 1) % array.shape[main_axis]] + place[main_axis + 1:]
    return array.at[tuple(place)].set(low).at[tuple(neighbour)].set(largest)


def steps_of(rng, shape, shards, smallest, largest):
    loudness, own = 1.0, jax.random.fold_in(rng, 6)
    for dim, shards_of in shards:
        heights = jnp.exp(jax.random.uniform(jax.random.fold_in(own, dim), (shards_of,), jnp.float32, smallest / len(shards), largest / len(shards)))
        loudness = loudness * jnp.repeat(heights, shape[dim] // shards_of).reshape([-1 if axis == dim else 1 for axis in range(len(shape))])
    return loudness


def length_profile(count, total, most, skew):
    loads = [(1 << 20) // math.isqrt(grade ** skew) + 1 for grade in range(2, count + 1)]
    rest, counts = total - most - (count - 1), [1] * (count - 1)
    while rest > 0:
        candidates = [i for i in range(count - 1) if counts[i] < most]
        pool, remaining = sum([loads[i] for i in candidates]), rest
        for i in candidates:
            more = min(most - counts[i], max(1, remaining * loads[i] // pool), rest)
            counts[i] = counts[i] + more
            rest = rest - more
    return np.array([most] + counts)


def ragged(own_key, number_of, total, most, skew):
    if number_of == 2:
        one = jax.random.randint(own_key, (), max(1, total - most), min(most, total - 1) + 1)
        return jnp.stack([one, total - one])
    tallies = jnp.asarray(length_profile(number_of, total, most, skew), jnp.int32)
    couples = (number_of - 1) // 2
    source_of, receiver = tallies[1:1 + 2 * couples:2], tallies[2:2 + 2 * couples:2]
    margin = jnp.minimum(source_of - 1, most - receiver)
    shifted = jax.random.randint(jax.random.fold_in(own_key, 1), (couples,), 0, 1 << 20) % (margin + 1)
    tallies = tallies.at[1:1 + 2 * couples:2].set(source_of - shifted).at[2:2 + 2 * couples:2].set(receiver + shifted)
    return tallies[jax.random.permutation(jax.random.fold_in(own_key, 2), number_of)]


def routed_block(key, own, number, rows, number_of, top, reach, lean):
    order = jax.random.permutation(key, number_of)
    crowded, usual = shares(number_of, rows * top, reach, lean, True), shares(number_of, rows * top, reach, lean, False)
    places = jnp.arange(number_of)

    def named(sizes, turn):
        used = int((sizes > 0).sum())
        fixed = max(1, used // 4)
        moved = fixed + (places - fixed + turn * (used - fixed)) % max(1, number_of - fixed)
        return jnp.zeros((number_of,), jnp.int32).at[order[jnp.where(places < fixed, places, moved)]].set(jnp.asarray(sizes, jnp.int32))

    sizes = jnp.where(number % 4 == 0, named(crowded, number // 4), named(usual, number - number // 4 - 1))
    mixed = jax.random.permutation(jax.random.fold_in(own, 3), number_of)
    source_of, taker = mixed[0:number_of // 2 * 2:2], mixed[1:number_of // 2 * 2:2]
    slack = jnp.minimum(sizes[source_of] - 1, reach - sizes[taker]) // 2
    slack = jnp.where((source_of == order[0]) | (taker == order[0]) | (sizes[taker] == 0), 0, jnp.maximum(slack, 0))
    moved = jax.random.randint(jax.random.fold_in(own, 4), (number_of // 2,), 0, 1 << 20) % (slack + 1)
    sizes = sizes.at[source_of].add(-moved).at[taker].add(moved)
    items = jnp.searchsorted(jnp.cumsum(sizes), jnp.arange(rows * top), side="right").astype(jnp.int32)
    grid = items.reshape(top, rows).T
    grid = grid[jax.random.permutation(jax.random.fold_in(own, 1), rows)]
    turn = jax.random.randint(jax.random.fold_in(own, 2), (rows, 1), 0, top)
    return jnp.take_along_axis(grid, (jnp.arange(top)[None, :] + turn) % top, axis=1)


def shares(count, total, reach, slope, full):
    loads = [(1 << 20) // math.isqrt(standing ** slope) + 1 for standing in range(1, count + 1)]
    largest = reach if full else min(reach, max(-(-total // count), total * loads[0] // sum(loads)))
    least = 1 if total - largest >= count - 1 else 0
    holding, rest = [largest] + [least] * (count - 1), total - largest - least * (count - 1)
    while rest > 0:
        movable = [i for i in range(1, count) if holding[i] < largest] or [i for i in range(1, count) if holding[i] < reach]
        mass, budget = sum([loads[i] for i in movable]), rest
        for i in movable:
            extra = min(reach - holding[i], max(1, budget * loads[i] // mass), rest)
            holding[i] = holding[i] + extra
            rest = rest - extra
    return np.array(holding)


def scatter_about(rng, dims, scale, reach, shards=(), kind=jnp.bfloat16):
    gain = steps_of(rng, dims, shards, -0.22, 0.18) if shards else 1.0
    array = jax.random.normal(rng, dims, jnp.float32) * scale * gain
    return jnp.minimum(jnp.maximum(array, -reach), reach).astype(kind)


def setup_inputs(seed: int = 0) -> dict:
    splits = jax.random.split(jax.random.key(seed), 12)
    q_nope = scatter_about(splits[0], (ROWS, STEPS, H, DN), 1.0, 6.0, ((0, 32), (2, 16)))
    q_rope = draw_q_rope(jax.random.fold_in(splits[11], 71), 0)
    new_latent = draw_new_latent(jax.random.fold_in(splits[11], 71), 0)
    w_uk = scatter_about(splits[3], (H, DN, DC), DN ** -0.5, 0.5, ((0, 16),))
    w_uv = scatter_about(splits[4], (H, DC, DV), 0.5, 3.0, ((0, 16),))
    prefix_store = scatter_about(splits[5], (GROUPS, PLEN, DC + DR), 1.0, 6.0, ((0, 32), (1, 16)))
    store_order = jax.random.permutation(splits[6], GROUPS).astype(jnp.int32)
    prefix_of_group = touch_ends(jax.random.randint(splits[7], (GROUPS,), 0, NPREF), jax.random.fold_in(splits[7], 1), 0, NPREF - 1).astype(jnp.int32)
    private_store = scatter_about(splits[8], (GROUPS, GROUPS, CAP, PRIV, DC + DR), 1.0, 6.0, ((0, 32), (3, 16)))
    request_source_keys = jax.random.split(jax.random.fold_in(splits[9], 1), ROWS // REQ)
    request_source_turns = jax.random.permutation(jax.random.fold_in(splits[9], 3), ROWS // REQ)
    request_source = jax.vmap(lambda own, number: routed_block(jax.random.fold_in(splits[9], 2), own, number, REQ, GROUPS, 1, CAP, 2))(request_source_keys, request_source_turns).reshape((ROWS, 1))
    private_len = jax.vmap(lambda own: ragged(own, REQ, REQ * PRIV * 3 // 4, PRIV, 2))(jax.random.split(splits[10], GROUPS)).reshape((GROUPS, REQ)).astype(jnp.int32)
    return dict(q_nope=q_nope, q_rope=q_rope, new_latent=new_latent, w_uk=w_uk, w_uv=w_uv, prefix_store=prefix_store, store_order=store_order, prefix_of_group=prefix_of_group, private_store=private_store, request_source=request_source, private_len=private_len)


score_scale = 192.0 ** -0.5
very_negative = -1.0e30


def rounded(value):
    return lax.optimization_barrier(value.astype(jnp.bfloat16)).astype(jnp.float32)


def one_group(group_id, q_nope, q_rope, new_latent, w_uk, w_uv, prefix_store, store_order, prefix_of_group, private_store, request_source, private_len):
    begin = group_id * REQ
    nope_rows = lax.dynamic_slice_in_dim(q_nope, begin, REQ, 0)
    rope_rows = lax.dynamic_slice_in_dim(q_rope, begin, REQ, 0).astype(jnp.float32)
    new_rows = lax.dynamic_slice_in_dim(new_latent, begin, REQ, 0).astype(jnp.float32)
    lat_rows = rounded(jnp.einsum('rthn,hnc->rthc', nope_rows.astype(jnp.float32), w_uk.astype(jnp.float32)))
    source_ids = lax.dynamic_slice_in_dim(request_source[:, 0], begin, REQ, 0).astype(jnp.int32)
    order_ids = jnp.arange(REQ, dtype=jnp.int32)
    earlier = (source_ids[:, None] == source_ids[None, :]) & (order_ids[None, :] < order_ids[:, None])
    slot_rank = jnp.sum(earlier, axis=1).astype(jnp.int32)
    private = private_store[source_ids, group_id, slot_rank].astype(jnp.float32)
    shared = prefix_store[store_order[prefix_of_group[group_id]]].astype(jnp.float32)
    lengths = private_len[group_id]
    prefix_scores = (jnp.einsum('rthc,kc->rthk', lat_rows, shared[:, :DC]) + jnp.einsum('rthc,kc->rthk', rope_rows, shared[:, DC:])) * score_scale
    private_scores = (jnp.einsum('rthc,rkc->rthk', lat_rows, private[..., :DC]) + jnp.einsum('rthc,rkc->rthk', rope_rows, private[..., DC:])) * score_scale
    new_scores = (jnp.einsum('rthc,rkc->rthk', lat_rows, new_rows[..., :DC]) + jnp.einsum('rthc,rkc->rthk', rope_rows, new_rows[..., DC:])) * score_scale
    private_usable = (jnp.arange(PRIV)[None, :] < lengths[:, None])[:, None, None, :]
    causal = (jnp.arange(STEPS)[:, None] >= jnp.arange(STEPS)[None, :])[None, :, None, :]
    private_scores = jnp.where(private_usable, private_scores, very_negative)
    new_scores = jnp.where(causal, new_scores, very_negative)
    top = jnp.maximum(jnp.max(prefix_scores, axis=-1), jnp.maximum(jnp.max(private_scores, axis=-1), jnp.max(new_scores, axis=-1)))
    prefix_exp = jnp.exp(prefix_scores - top[..., None])
    private_exp = jnp.where(private_usable, jnp.exp(private_scores - top[..., None]), 0.0)
    new_exp = jnp.where(causal, jnp.exp(new_scores - top[..., None]), 0.0)
    denominator = jnp.sum(prefix_exp, axis=-1) + jnp.sum(private_exp, axis=-1) + jnp.sum(new_exp, axis=-1)
    weighted = jnp.einsum('rthk,kc->rthc', rounded(prefix_exp), shared[:, :DC])
    weighted = weighted + jnp.einsum('rthk,rkc->rthc', rounded(private_exp), private[..., :DC])
    weighted = weighted + jnp.einsum('rthk,rkc->rthc', rounded(new_exp), new_rows[..., :DC])
    attended = rounded(weighted / denominator[..., None])
    return jnp.einsum('rthc,hcv->rthv', attended, w_uv.astype(jnp.float32)).astype(jnp.bfloat16)


def reference(q_nope, q_rope, new_latent, w_uk, w_uv, prefix_store, store_order, prefix_of_group, private_store, request_source, private_len):
    def run_group(group_id):
        return one_group(group_id, q_nope, q_rope, new_latent, w_uk, w_uv, prefix_store, store_order, prefix_of_group, private_store, request_source, private_len)

    outputs = lax.map(run_group, jnp.arange(GROUPS, dtype=jnp.int32))
    return outputs.reshape(GROUPS * REQ, STEPS, H, DV)
```

```python
import jax
import jax.numpy as jnp
from jax import lax
from jax.sharding import PartitionSpec as P

NPREF = 4

score_scale = 192.0 ** (-0.5)
very_negative = -1e30


def spread_prefix(prefix_shard, store_order, prefix_of_group, groups):
    rows, width = prefix_shard.shape
    pieces = prefix_shard.reshape(groups, rows // groups * width)
    arrived = lax.all_to_all(pieces, "rep", split_axis=0, concat_axis=0, tiled=True)
    chosen = arrived[store_order[prefix_of_group]]
    mine = lax.all_to_all(chosen, "rep", split_axis=0, concat_axis=0, tiled=True)
    return mine.reshape(rows, width)


def in_three(value):
    high = lax.reduce_precision(value, 8, 7)
    middle = lax.reduce_precision(value - high, 8, 7)
    low = value - high - middle
    return [part.astype(jnp.bfloat16) for part in (high, middle, low)]


def private_part(q, keys, new_keys, lengths, latent_width):
    owned, steps, heads, _ = q.shape
    scores = jnp.einsum("rthc,rkc->rthk", q, keys, preferred_element_type=jnp.float32) * score_scale
    positions = jnp.arange(keys.shape[1], dtype=jnp.int32)
    usable = (positions[None, :] < lengths[:, None])[:, None, None, :]
    scores = jnp.where(usable, scores, very_negative)
    new_scores = jnp.einsum("rthc,rkc->rthk", q, new_keys, preferred_element_type=jnp.float32) * score_scale
    causal = (jnp.arange(steps)[:, None] >= jnp.arange(steps)[None, :])[None, :, None, :]
    new_scores = jnp.where(causal, new_scores, very_negative)
    top = jnp.maximum(jnp.max(scores, axis=-1), jnp.max(new_scores, axis=-1))
    e = jnp.where(usable, jnp.exp(scores - top[..., None]), 0.0)
    new_e = jnp.where(causal, jnp.exp(new_scores - top[..., None]), 0.0)
    total = jnp.sum(e, axis=-1) + jnp.sum(new_e, axis=-1)
    weighted = jnp.einsum(
        "rthk,rkc->rthc", e.astype(jnp.bfloat16), keys[..., :latent_width], preferred_element_type=jnp.float32
    ) + jnp.einsum(
        "rthk,rkc->rthc", new_e.astype(jnp.bfloat16), new_keys[..., :latent_width], preferred_element_type=jnp.float32
    )
    return weighted / total[..., None], top + jnp.log(total)


def shards(
    q_nope,
    q_rope,
    new_latent,
    w_uk,
    w_uv,
    prefix_store,
    store_order,
    prefix_of_group,
    private_store,
    request_source,
    private_len,
):
    latent_width = w_uk.shape[2]
    requests, steps, heads = (q_nope.shape[0], q_nope.shape[1], q_nope.shape[2])
    groups, capacity = private_store.shape[1], private_store.shape[2]
    q_lat = jnp.einsum("rthn,hnc->rthc", q_nope, w_uk, preferred_element_type=jnp.float32).astype(
        jnp.bfloat16
    )
    q = jnp.concatenate([q_lat, q_rope], axis=-1)

    received = lax.all_to_all(private_store, "rep", split_axis=1, concat_axis=0, tiled=True)
    received = received.reshape(-1, received.shape[3], received.shape[4])
    source_ids = request_source[:, 0]
    order_ids = jnp.arange(requests, dtype=jnp.int32)
    earlier = (source_ids[:, None] == source_ids[None, :]) & (
        order_ids[None, :] < order_ids[:, None]
    )
    slot_index = source_ids * capacity + jnp.sum(earlier, axis=1)
    pages = lax.all_to_all(received[slot_index], "grp", split_axis=0, concat_axis=1, tiled=True)
    owned = pages.shape[0]

    q_owned = lax.all_to_all(q, "grp", split_axis=0, concat_axis=2, tiled=True)
    first = lax.axis_index("grp") * owned
    new_keys = lax.dynamic_slice_in_dim(new_latent, first, owned, 0)
    lengths = lax.dynamic_slice_in_dim(private_len[0], first, owned, 0)
    part, part_lse = private_part(q_owned, pages, new_keys, lengths, latent_width)
    back = jnp.concatenate([part.astype(jnp.bfloat16)] + [x[..., None] for x in in_three(part_lse)], axis=-1)
    back = lax.all_to_all(back, "grp", split_axis=2, concat_axis=0, tiled=True)
    part = back[..., :latent_width].astype(jnp.float32)
    part_lse = jnp.sum(back[..., latent_width:].astype(jnp.float32), axis=-1)

    shard = spread_prefix(prefix_store[0], store_order, prefix_of_group, groups)
    shared = lax.all_gather(shard, "grp", axis=0, tiled=True)
    scores = jnp.einsum("rthc,kc->rthk", q, shared, preferred_element_type=jnp.float32) * score_scale
    top = jnp.max(scores, axis=-1)
    e = jnp.exp(scores - top[..., None])
    total = jnp.sum(e, axis=-1)
    weighted = jnp.einsum(
        "rthk,kc->rthc", e.astype(jnp.bfloat16), shared[:, :latent_width], preferred_element_type=jnp.float32
    )
    both = jnp.maximum(top, part_lse)
    scale, part_scale = jnp.exp(top - both), jnp.exp(part_lse - both)
    attended = (weighted * scale[..., None] + part * part_scale[..., None]) / (total * scale + part_scale)[..., None]
    return jnp.einsum(
        "rthc,hcv->rthv", attended.astype(jnp.bfloat16), w_uv, preferred_element_type=jnp.float32
    ).astype(jnp.bfloat16)


def solution(mesh):
    in_specs = (
        P("rep", None, "grp", None),
        P("rep", None, "grp", None),
        P("rep", None, None),
        P("grp", None, None),
        P("grp", None, None),
        P("rep", "grp", None),
        P(),
        P(),
        P("rep", None, None, "grp", None),
        P("rep", None),
        P("rep", None),
    )
    out_specs = P("rep", None, "grp", None)
    return jax.shard_map(shards, mesh=mesh, in_specs=in_specs, out_specs=out_specs, check_vma=False)
```

```python
import functools

import jax
import jax.numpy as jnp
from jax import lax
from jax.experimental import pallas as pl
from jax.experimental.pallas import tpu as pltpu
from jax.sharding import PartitionSpec as P

score_scale = 192.0 ** (-0.5)
very_negative = -1e30
MIB = 1024 * 1024
MESH = pl.DeviceIdType.MESH


def contract_last(a, b):
    return lax.dot_general(a, b, (((1,), (1,)), ((), ())), preferred_element_type=jnp.float32)


def loop(count, body):
    def step(i, carry):
        body(i)
        return carry

    lax.fori_loop(0, count, step, 0)


def remote(src, dst, send, recv, where):
    return pltpu.make_async_remote_copy(
        src_ref=src, dst_ref=dst, send_sem=send, recv_sem=recv, device_id=where, device_id_type=MESH
    )


def greet(groups, members):
    me, mine = lax.axis_index("rep"), lax.axis_index("grp")
    barrier = pltpu.get_barrier_semaphore()

    def along_rep(k):
        pl.semaphore_signal(barrier, inc=1, device_id={"rep": (me + k + 1) % groups}, device_id_type=MESH)

    def along_grp(k):
        pl.semaphore_signal(barrier, inc=1, device_id={"grp": (mine + k + 1) % members}, device_id_type=MESH)

    loop(groups - 1, along_rep)
    loop(members - 1, along_grp)
    pl.semaphore_wait(barrier, groups + members - 2)


class Exchange:
    def __init__(self, axis, peers, out_ref, in_ref, send, recv):
        self.axis, self.peers, self.out_ref, self.in_ref, self.send, self.recv = axis, peers, out_ref, in_ref, send, recv
        self.me = lax.axis_index(axis)

    def peer(self, k):
        return (self.me + k + 1) % self.peers

    def to(self, j):
        return remote(self.out_ref(j), self.in_ref(self.me), self.send(j), self.recv(self.me), {self.axis: j})

    def own(self):
        return pltpu.make_async_copy(self.out_ref(self.me), self.in_ref(self.me), self.recv(self.me))

    def start(self, begin=0, end=None):
        loop((self.peers - 1 if end is None else end) - begin, lambda k: self.to(self.peer(k + begin)).start())

    def arrive(self, j):
        remote(self.out_ref(j), self.in_ref(j), self.send(j), self.recv(j), {self.axis: j}).wait_recv()

    def finish(self):
        self.own().wait()
        loop(self.peers - 1, lambda k: self.arrive(self.peer(k)))

    def drain(self):
        loop(self.peers - 1, lambda k: self.to(self.peer(k)).wait_send())


def prefix_kernel(
    groups,
    members,
    q_lat,
    q_rope,
    store_lat,
    store_rope,
    store_order,
    prefix_of_group,
    out,
    top,
    total,
    one_out,
    one_in,
    two_out,
    two_in,
    pref_lat,
    pref_rope,
    scores,
    one_send,
    one_recv,
    two_send,
    two_recv,
    ring_send,
    ring_recv,
    ring_rope_send,
    ring_rope_recv,
):
    mine = lax.axis_index("grp")
    half = members // 2
    z, y = mine // 2, mine % 2
    latent, rope = q_lat.shape[1], q_rope.shape[1]
    lanes = latent // 4

    def rows_of(j):
        return pl.ds(pl.multiple_of((j // 4) * 16, 16), 16)

    def columns_of(j):
        return pl.ds(pl.multiple_of((j % 4) * lanes, lanes), lanes)

    def cut(j):
        one_out[j, pl.ds(0, 16)] = store_lat[rows_of(j), columns_of(j)]
        one_out[j, pl.ds(16, 16)] = jnp.concatenate([store_rope[rows_of(j)], jnp.zeros((16, lanes - rope), jnp.bfloat16)], axis=1)

    loop(groups, cut)
    greet(groups, members)
    one = Exchange("rep", groups, lambda j: one_out.at[j], lambda j: one_in.at[j], lambda j: one_send.at[j], lambda j: one_recv.at[j])
    two = Exchange("rep", groups, lambda j: two_out.at[j], lambda j: two_in.at[j], lambda j: two_send.at[j], lambda j: two_recv.at[j])
    one.start()
    one.own().start()
    one.finish()

    def choose(j):
        two_out[j] = one_in[store_order[prefix_of_group[j]]]

    loop(groups, choose)
    two.start()
    two.own().start()
    two.finish()

    def place(j):
        pref_lat[mine, rows_of(j), columns_of(j)] = two_in[j, pl.ds(0, 16)]

    def place_rope(b):
        pref_rope[mine, pl.ds(pl.multiple_of(b * 16, 16), 16)] = two_in[4 * b, pl.ds(16, 16), pl.ds(0, rope)]

    loop(groups, place)
    loop(groups // 4, place_rope)

    across = {"grp": z * 2 + 1 - y}
    up, down = {"grp": ((z + 1) % half) * 2 + y}, {"grp": ((z + half - 1) % half) * 2 + y}

    def shard_of(dz, column):
        return ((z + dz + half) % half) * 2 + column

    def ring(c, way, where):
        return (
            remote(pref_lat.at[c], pref_lat.at[c], ring_send.at[way, c], ring_recv.at[c], where),
            remote(pref_rope.at[c], pref_rope.at[c], ring_rope_send.at[way, c], ring_rope_recv.at[c], where),
        )

    def send_on(c, way, where):
        for copy in ring(c, way, where):
            copy.start()

    def arrived(c):
        for copy in ring(c, 0, up):
            copy.wait_recv()

    def sent(c, way, where):
        for copy in ring(c, way, where):
            copy.wait_send()

    other = shard_of(0, 1 - y)
    send_on(mine, 0, up)
    send_on(mine, 1, down)
    send_on(mine, 2, across)
    arrived(other)
    send_on(other, 0, up)
    send_on(other, 1, down)
    for hop in (1, 2, 3):
        for column in (0, 1):
            c = shard_of(-hop, column)
            arrived(c)
            if hop < 3 or column == 0:
                send_on(c, 0, up)
            c = shard_of(hop, column)
            arrived(c)
            if hop < 3 or column == 1:
                send_on(c, 1, down)
    for column in (0, 1):
        arrived(shard_of(4, column))

    tiles, tile = scores.shape[0], scores.shape[2]
    top[...] = jnp.full_like(top, very_negative)
    total[...] = jnp.zeros_like(total)
    out[...] = jnp.zeros_like(out)

    def score(i):
        k_lat = pref_lat[pl.ds(2 * i, 2)].reshape(tile, latent)
        k_rope = pref_rope[pl.ds(2 * i, 2)].reshape(tile, rope)
        s = (contract_last(q_lat[...], k_lat) + contract_last(q_rope[...], k_rope)) * score_scale
        scores[i] = s
        top[...] = jnp.maximum(top[...], jnp.max(s, axis=1, keepdims=True))

    loop(tiles, score)

    def weigh(i):
        e = jnp.exp(scores[i] - top[...])
        total[...] += jnp.sum(e, axis=1, keepdims=True)
        k_lat = pref_lat[pl.ds(2 * i, 2)].reshape(tile, latent)
        out[...] += jnp.dot(e.astype(jnp.bfloat16), k_lat, preferred_element_type=jnp.float32)

    loop(tiles, weigh)
    one.drain()
    two.drain()
    sent(mine, 0, up)
    sent(mine, 1, down)
    sent(mine, 2, across)
    sent(other, 0, up)
    sent(other, 1, down)
    for hop in (1, 2, 3):
        for column in (0, 1):
            if hop < 3 or column == 0:
                sent(shard_of(-hop, column), 0, up)
            if hop < 3 or column == 1:
                sent(shard_of(hop, column), 1, down)


def prefix_attention(members, q_lat, q_rope, prefix_shard, store_order, prefix_of_group):
    groups = store_order.shape[0]
    rows, latent = q_lat.shape
    rope = q_rope.shape[1]
    shard = prefix_shard.shape[0]
    lanes = latent // 4
    bf16, f32 = jnp.bfloat16, jnp.float32
    vmem, smem = pl.BlockSpec(memory_space=pltpu.VMEM), pl.BlockSpec(memory_space=pltpu.SMEM)
    dma = pltpu.SemaphoreType.DMA
    return pl.pallas_call(
        functools.partial(prefix_kernel, groups, members),
        out_shape=[
            jax.ShapeDtypeStruct((rows, latent), f32),
            jax.ShapeDtypeStruct((rows, 1), f32),
            jax.ShapeDtypeStruct((rows, 1), f32),
        ],
        in_specs=[vmem, vmem, vmem, vmem, smem, smem],
        out_specs=[vmem, vmem, vmem],
        scratch_shapes=[pltpu.VMEM((groups, 32, lanes), bf16)] * 4
        + [
            pltpu.VMEM((members, shard, latent), bf16),
            pltpu.VMEM((members, shard, rope), bf16),
            pltpu.VMEM((members // 2, rows, 2 * shard), f32),
        ]
        + [dma((groups,))] * 4
        + [dma((3, members)), dma((members,)), dma((3, members)), dma((members,))],
        compiler_params=pltpu.CompilerParams(collective_id=0, has_side_effects=True, vmem_limit_bytes=40 * MIB),
        cost_estimate=pl.CostEstimate(flops=2_300_000_000, bytes_accessed=4_000_000, transcendentals=1_000_000),
    )(q_lat, q_rope, prefix_shard[:, :latent], prefix_shard[:, latent:], store_order, prefix_of_group)


def private_kernel(
    groups,
    members,
    q_lat,
    q_rope,
    new_latent,
    private_store,
    request_source,
    private_len,
    prefix_out,
    prefix_top,
    prefix_total,
    out,
    pages_in,
    pages_out,
    keys,
    ql_in,
    qr_in,
    part_out,
    part_in,
    slots,
    pages_send,
    pages_recv,
    keys_send,
    keys_recv,
    ql_send,
    ql_recv,
    qr_send,
    qr_recv,
    part_send,
    part_recv,
):
    me, mine = lax.axis_index("rep"), lax.axis_index("grp")
    requests = request_source.shape[0]
    owned = requests // members
    latent, rope = q_lat.shape[1], q_rope.shape[1]
    lanes = latent // 4
    capacity, depth = private_store.shape[1:3]
    own_rows = q_lat.shape[0] // members
    block = own_rows // owned
    greet(groups, members)

    def query_rows(j):
        return pl.ds(pl.multiple_of(j * own_rows, own_rows), own_rows)

    pages = Exchange("rep", groups, lambda j: private_store.at[j], lambda j: pages_in.at[j], lambda j: pages_send.at[j], lambda j: pages_recv.at[j])
    ql = Exchange("grp", members, lambda j: q_lat.at[query_rows(j)], lambda j: ql_in.at[j], lambda j: ql_send.at[j], lambda j: ql_recv.at[j])
    qr = Exchange("grp", members, lambda j: q_rope.at[query_rows(j)], lambda j: qr_in.at[j], lambda j: qr_send.at[j], lambda j: qr_recv.at[j])

    def key_exchange(a):
        return Exchange(
            "grp", members, lambda j: pages_out.at[j * owned + a], lambda j: keys.at[a, j], lambda j: keys_send.at[a, j], lambda j: keys_recv.at[a, j]
        )

    def part_exchange(a):
        return Exchange(
            "grp", members, lambda j: part_out.at[a, j], lambda j: part_in.at[a, j], lambda j: part_send.at[a, j], lambda j: part_recv.at[a, j]
        )

    @pl.when(me % 2 == 0)
    def _():
        pages.start()
        ql.start()
        qr.start()

    @pl.when(me % 2 == 1)
    def _():
        ql.start()
        qr.start()
        pages.start()

    pages.own().start()
    ql.own().start()
    qr.own().start()

    def find_slot(i):
        source = request_source[i]

        def count(j, rank):
            return rank + jnp.where((request_source[j] == source) & (j < i), 1, 0)

        slots[i] = jnp.minimum(lax.fori_loop(0, requests, count, jnp.int32(0)), capacity - 1)

    loop(requests, find_slot)
    pages.finish()

    def pick(i):
        pages_out[i] = pages_in[request_source[i], slots[i]]

    loop(requests, pick)
    for a in range(owned):
        key_exchange(a).start()
        key_exchange(a).own().start()
    ql.finish()
    qr.finish()

    def attend(a):
        rows = members * block
        at = pl.ds(pl.multiple_of(a * block, block), block)
        q_l = ql_in[:, at, :].reshape(rows, latent)
        q_r = qr_in[:, at, :].reshape(rows, rope)
        k = keys[a].reshape(members * depth, keys.shape[3])
        k_lat, k_rope = k[:, :latent], k[:, latent:]
        s = (contract_last(q_l, k_lat) + contract_last(q_r, k_rope)) * score_scale
        usable = lax.broadcasted_iota(jnp.int32, s.shape, 1) < private_len[mine * owned + a]
        s = jnp.where(usable, s, very_negative)
        fresh = new_latent[mine * owned + a].astype(jnp.float32)
        q_l32, q_r32 = q_l.astype(jnp.float32), q_r.astype(jnp.float32)
        step = (lax.broadcasted_iota(jnp.int32, (rows, 1), 0) % block) // (block // 2)
        new_s = []
        for u in range(2):
            row = fresh[u : u + 1]
            s_u = (
                jnp.sum(q_l32 * row[:, :latent], axis=1, keepdims=True) + jnp.sum(q_r32 * row[:, latent:], axis=1, keepdims=True)
            ) * score_scale
            new_s.append(jnp.where(step >= u, s_u, very_negative))
        m = jnp.maximum(jnp.max(s, axis=1, keepdims=True), jnp.maximum(new_s[0], new_s[1]))
        e = jnp.where(usable, jnp.exp(s - m), 0.0)
        length = jnp.sum(e, axis=1, keepdims=True)
        weighted = jnp.dot(e.astype(jnp.bfloat16), k_lat, preferred_element_type=jnp.float32)
        for u in range(2):
            e_u = jnp.where(step >= u, jnp.exp(new_s[u] - m), 0.0)
            length = length + e_u
            weighted = weighted + e_u.astype(jnp.bfloat16).astype(jnp.float32) * fresh[u : u + 1, :latent]
        lse = m + jnp.log(length)
        high = lse.astype(jnp.bfloat16).astype(jnp.float32)
        middle = (lse - high).astype(jnp.bfloat16).astype(jnp.float32)
        low = lse - high - middle
        place = lax.broadcasted_iota(jnp.int32, (rows, lanes), 1)
        tail = jnp.where(place == 0, high, jnp.where(place == 1, middle, jnp.where(place == 2, low, 0.0)))
        part_out[a, :, :, pl.ds(0, latent)] = (weighted / length).astype(jnp.bfloat16).reshape(members, block, latent)
        part_out[a, :, :, pl.ds(latent, lanes)] = tail.astype(jnp.bfloat16).reshape(members, block, lanes)

    def attend_and_send(a):
        key_exchange(a).finish()
        attend(a)
        part_exchange(a).start()
        part_exchange(a).own().start()

    loop(owned, attend_and_send)

    def merge(a, j):
        rows = pl.ds(pl.multiple_of(j * own_rows + a * block, block), block)
        tail = part_in[a, j, :, pl.ds(latent, lanes)].astype(jnp.float32)
        lse = jnp.sum(tail, axis=1, keepdims=True)
        part = part_in[a, j, :, pl.ds(0, latent)].astype(jnp.float32)
        top = prefix_top[rows]
        m = jnp.maximum(top, lse)
        scale, part_scale = jnp.exp(top - m), jnp.exp(lse - m)
        length = prefix_total[rows] * scale + part_scale
        out[rows] = ((prefix_out[rows] * scale + part * part_scale) / length).astype(jnp.bfloat16)

    def merge_all(a):
        part_exchange(a).finish()
        loop(members, lambda j: merge(a, j))

    loop(owned, merge_all)
    pages.drain()
    ql.drain()
    qr.drain()
    for a in range(owned):
        key_exchange(a).drain()
        part_exchange(a).drain()


def private_attention(members, q_lat, q_rope, new_latent, private_store, request_source, private_len, prefix_out, prefix_top, prefix_total):
    groups, capacity, depth, width = private_store.shape
    rows, latent = q_lat.shape
    rope = q_rope.shape[1]
    requests = new_latent.shape[0]
    owned = requests // members
    own = rows // members
    lanes = latent // 4
    bf16 = jnp.bfloat16
    vmem, smem, anywhere = [pl.BlockSpec(memory_space=m) for m in (pltpu.VMEM, pltpu.SMEM, pl.ANY)]
    dma = pltpu.SemaphoreType.DMA
    return pl.pallas_call(
        functools.partial(private_kernel, groups, members),
        out_shape=jax.ShapeDtypeStruct((rows, latent), bf16),
        in_specs=[vmem, vmem, vmem, anywhere, smem, smem, vmem, vmem, vmem],
        out_specs=vmem,
        scratch_shapes=[
            pltpu.VMEM((groups, capacity, depth, width), bf16),
            pltpu.VMEM((requests, depth, width), bf16),
            pltpu.VMEM((owned, members, depth, width), bf16),
            pltpu.VMEM((members, own, latent), bf16),
            pltpu.VMEM((members, own, rope), bf16),
            pltpu.VMEM((owned, members, own // owned, latent + lanes), bf16),
            pltpu.VMEM((owned, members, own // owned, latent + lanes), bf16),
            pltpu.SMEM((requests,), jnp.int32),
            dma((groups,)),
            dma((groups,)),
            dma((owned, members)),
            dma((owned, members)),
            dma((members,)),
            dma((members,)),
            dma((members,)),
            dma((members,)),
            dma((owned, members)),
            dma((owned, members)),
        ],
        compiler_params=pltpu.CompilerParams(collective_id=1, has_side_effects=True, vmem_limit_bytes=40 * MIB),
        cost_estimate=pl.CostEstimate(flops=400_000_000, bytes_accessed=8_000_000, transcendentals=1_000_000),
    )(q_lat, q_rope, new_latent, private_store, request_source, private_len, prefix_out, prefix_top, prefix_total)


def shards(
    members,
    q_nope,
    q_rope,
    new_latent,
    w_uk,
    w_uv,
    prefix_store,
    store_order,
    prefix_of_group,
    private_store,
    request_source,
    private_len,
):
    requests, steps, heads = q_nope.shape[:3]
    rows = requests * steps * heads
    q_lat = jnp.einsum("rthn,hnc->rthc", q_nope, w_uk, preferred_element_type=jnp.float32).astype(jnp.bfloat16)
    q_lat, q_rope = q_lat.reshape(rows, -1), q_rope.reshape(rows, -1)
    prefix = prefix_attention(members, q_lat, q_rope, prefix_store[0], store_order, prefix_of_group)
    attended = private_attention(members, q_lat, q_rope, new_latent, private_store[0], request_source[:, 0], private_len[0], *prefix)
    attended = attended.reshape(requests, steps, heads, -1)
    return jnp.einsum("rthc,hcv->rthv", attended, w_uv, preferred_element_type=jnp.float32).astype(jnp.bfloat16)


def solution(mesh):
    in_specs = (
        P("rep", None, "grp", None),
        P("rep", None, "grp", None),
        P("rep", None, None),
        P("grp", None, None),
        P("grp", None, None),
        P("rep", "grp", None),
        P(),
        P(),
        P("rep", None, None, "grp", None),
        P("rep", None),
        P("rep", None),
    )
    out_specs = P("rep", None, "grp", None)
    body = functools.partial(shards, mesh.shape["grp"])
    return jax.shard_map(body, mesh=mesh, in_specs=in_specs, out_specs=out_specs, check_vma=False)
```

```python
import functools

import jax
import jax.numpy as jnp
from jax import lax
from jax.experimental import pallas as pl
from jax.experimental.pallas import tpu as pltpu
from jax.sharding import PartitionSpec as P

score_scale = 192.0 ** (-0.5)
very_negative = -1e30
MIB = 1024 * 1024
MESH = pl.DeviceIdType.MESH
EARLY = 12
ATTEND_AFTER = 3


def contract_last(a, b):
    return lax.dot_general(a, b, (((1,), (1,)), ((), ())), preferred_element_type=jnp.float32)


def loop(count, body):
    def step(i, carry):
        body(i)
        return carry

    lax.fori_loop(0, count, step, 0)


def remote(src, dst, send, recv, where):
    return pltpu.make_async_remote_copy(
        src_ref=src, dst_ref=dst, send_sem=send, recv_sem=recv, device_id=where, device_id_type=MESH
    )


def greet(groups, members):
    me, mine = lax.axis_index("rep"), lax.axis_index("grp")
    barrier = pltpu.get_barrier_semaphore()

    def along_rep(k):
        pl.semaphore_signal(barrier, inc=1, device_id={"rep": (me + k + 1) % groups}, device_id_type=MESH)

    def along_grp(k):
        pl.semaphore_signal(barrier, inc=1, device_id={"grp": (mine + k + 1) % members}, device_id_type=MESH)

    loop(groups - 1, along_rep)
    loop(members - 1, along_grp)
    pl.semaphore_wait(barrier, groups + members - 2)


class Exchange:
    def __init__(self, axis, peers, out_ref, in_ref, send, recv):
        self.axis, self.peers, self.out_ref, self.in_ref, self.send, self.recv = axis, peers, out_ref, in_ref, send, recv
        self.me = lax.axis_index(axis)

    def peer(self, k):
        return (self.me + k + 1) % self.peers

    def to(self, j):
        return remote(self.out_ref(j), self.in_ref(self.me), self.send(j), self.recv(self.me), {self.axis: j})

    def own(self):
        return pltpu.make_async_copy(self.out_ref(self.me), self.in_ref(self.me), self.recv(self.me))

    def start(self, begin=0, end=None):
        loop((self.peers - 1 if end is None else end) - begin, lambda k: self.to(self.peer(k + begin)).start())

    def arrive(self, j):
        remote(self.out_ref(j), self.in_ref(j), self.send(j), self.recv(j), {self.axis: j}).wait_recv()

    def finish(self):
        self.own().wait()
        loop(self.peers - 1, lambda k: self.arrive(self.peer(k)))

    def drain(self):
        loop(self.peers - 1, lambda k: self.to(self.peer(k)).wait_send())


def kernel(
    groups,
    members,
    q_lat,
    q_rope,
    new_latent,
    store_lat,
    store_rope,
    store_order,
    prefix_of_group,
    private_store,
    request_source,
    private_len,
    out,
    q_out,
    q_in,
    one_out,
    one_in,
    two_out,
    two_in,
    pref,
    scores,
    weighted,
    top,
    total,
    pages_in,
    pages_out,
    keys,
    part_out,
    part_in,
    slots,
    one_send,
    one_recv,
    two_send,
    two_recv,
    ring_send,
    ring_recv,
    pages_send,
    pages_recv,
    keys_send,
    keys_recv,
    q_send,
    q_recv,
    part_send,
    part_recv,
):
    me, mine = lax.axis_index("rep"), lax.axis_index("grp")
    half = members // 2
    z, y = mine // 2, mine % 2
    latent, rope = q_lat.shape[1], q_rope.shape[1]
    lanes = latent // 4
    requests = request_source.shape[0]
    owned = requests // members
    capacity, depth = private_store.shape[1:3]
    own_rows = q_lat.shape[0] // members
    block = own_rows // owned

    def rows_of(j):
        return pl.ds(pl.multiple_of((j // 4) * 16, 16), 16)

    def columns_of(j):
        return pl.ds(pl.multiple_of((j % 4) * lanes, lanes), lanes)

    def cut(j):
        one_out[j, pl.ds(0, 16)] = store_lat[rows_of(j), columns_of(j)]
        one_out[j, pl.ds(16, 16)] = jnp.concatenate([store_rope[rows_of(j)], jnp.zeros((16, lanes - rope), jnp.bfloat16)], axis=1)

    loop(groups, cut)

    def query_rows(j):
        return pl.ds(pl.multiple_of(j * own_rows, own_rows), own_rows)

    def put_query(j):
        q_out[j, :, pl.ds(0, latent)] = q_lat[query_rows(j)]
        q_out[j, :, pl.ds(latent, lanes)] = jnp.concatenate(
            [q_rope[query_rows(j)], jnp.zeros((own_rows, lanes - rope), jnp.bfloat16)], axis=1
        )

    loop(members, put_query)
    greet(groups, members)
    one = Exchange("rep", groups, lambda j: one_out.at[j], lambda j: one_in.at[j], lambda j: one_send.at[j], lambda j: one_recv.at[j])
    two = Exchange("rep", groups, lambda j: two_out.at[j], lambda j: two_in.at[j], lambda j: two_send.at[j], lambda j: two_recv.at[j])
    pages = Exchange("rep", groups, lambda j: private_store.at[j], lambda j: pages_in.at[j], lambda j: pages_send.at[j], lambda j: pages_recv.at[j])
    queries = Exchange("grp", members, lambda j: q_out.at[j], lambda j: q_in.at[j], lambda j: q_send.at[j], lambda j: q_recv.at[j])

    def key_exchange(a):
        return Exchange(
            "grp", members, lambda j: pages_out.at[j * owned + a], lambda j: keys.at[a, j], lambda j: keys_send.at[a, j], lambda j: keys_recv.at[a, j]
        )

    def part_exchange(a):
        return Exchange(
            "grp", members, lambda j: part_out.at[a, j], lambda j: part_in.at[a, j], lambda j: part_send.at[a, j], lambda j: part_recv.at[a, j]
        )

    one.start()
    one.own().start()

    @pl.when(me % 2 == 1)
    def _():
        queries.start()

    pages.start(0, EARLY)
    pages.own().start()
    queries.own().start()
    one.finish()

    def choose(j):
        two_out[j] = one_in[store_order[prefix_of_group[j]]]

    loop(groups, choose)
    two.start()
    two.own().start()
    pages.start(EARLY, groups - 1)

    @pl.when(me % 2 == 0)
    def _():
        queries.start()


    def find_slot(i):
        source = request_source[i]

        def count(j, rank):
            return rank + jnp.where((request_source[j] == source) & (j < i), 1, 0)

        slots[i] = jnp.minimum(lax.fori_loop(0, requests, count, jnp.int32(0)), capacity - 1)

    loop(requests, find_slot)
    pages.finish()

    def pick(i):
        pages_out[i] = pages_in[request_source[i], slots[i]]

    loop(requests, pick)
    for a in range(owned):
        key_exchange(a).start()
        key_exchange(a).own().start()
    two.finish()

    def place(j):
        pref[mine, rows_of(j), columns_of(j)] = two_in[j, pl.ds(0, 16)]

    def place_rope(b):
        pref[mine, pl.ds(pl.multiple_of(b * 16, 16), 16), pl.ds(latent, lanes)] = two_in[4 * b, pl.ds(16, 16)]

    loop(groups, place)
    loop(groups // 4, place_rope)

    across = {"grp": z * 2 + 1 - y}
    up, down = {"grp": ((z + 1) % half) * 2 + y}, {"grp": ((z + half - 1) % half) * 2 + y}

    def shard_of(dz, column):
        return ((z + dz + half) % half) * 2 + column

    def ring(c, way, where):
        return remote(pref.at[c], pref.at[c], ring_send.at[way, c], ring_recv.at[c], where)

    def arrived(c):
        ring(c, 0, up).wait_recv()

    sends = []

    def send_on(c, way, where):
        ring(c, way, where).start()
        sends.append((c, way, where))

    other = shard_of(0, 1 - y)
    send_on(mine, 0, up)
    send_on(mine, 1, down)
    send_on(mine, 2, across)
    width = pref.shape[2]

    def attend(a):
        rows = members * block
        at = pl.ds(pl.multiple_of(a * block, block), block)
        q = q_in[:, at, :].reshape(rows, width)[:, : latent + rope]
        k = keys[a].reshape(members * depth, latent + rope)
        s = contract_last(q, k) * score_scale
        usable = lax.broadcasted_iota(jnp.int32, s.shape, 1) < private_len[mine * owned + a]
        s = jnp.where(usable, s, very_negative)
        fresh = new_latent[mine * owned + a].astype(jnp.float32)
        q32 = q.astype(jnp.float32)
        step = (lax.broadcasted_iota(jnp.int32, (rows, 1), 0) % block) // (block // 2)
        new_s = []
        for u in range(2):
            s_u = jnp.sum(q32 * fresh[u : u + 1], axis=1, keepdims=True) * score_scale
            new_s.append(jnp.where(step >= u, s_u, very_negative))
        m = jnp.maximum(jnp.max(s, axis=1, keepdims=True), jnp.maximum(new_s[0], new_s[1]))
        e = jnp.where(usable, jnp.exp(s - m), 0.0)
        length = jnp.sum(e, axis=1, keepdims=True)
        summed = jnp.dot(e.astype(jnp.bfloat16), k[:, :latent], preferred_element_type=jnp.float32)
        for u in range(2):
            e_u = jnp.where(step >= u, jnp.exp(new_s[u] - m), 0.0)
            length = length + e_u
            summed = summed + e_u.astype(jnp.bfloat16).astype(jnp.float32) * fresh[u : u + 1, :latent]
        lse = m + jnp.log(length)
        high = lse.astype(jnp.bfloat16).astype(jnp.float32)
        middle = (lse - high).astype(jnp.bfloat16).astype(jnp.float32)
        low = lse - high - middle
        place = lax.broadcasted_iota(jnp.int32, (rows, lanes), 1)
        tail = jnp.where(place == 0, high, jnp.where(place == 1, middle, jnp.where(place == 2, low, 0.0)))
        part_out[a, :, :, pl.ds(0, latent)] = (summed / length).astype(jnp.bfloat16).reshape(members, block, latent)
        part_out[a, :, :, pl.ds(latent, lanes)] = tail.astype(jnp.bfloat16).reshape(members, block, lanes)

    def attend_and_send(a):
        key_exchange(a).finish()
        attend(a)
        part_exchange(a).start()
        part_exchange(a).own().start()

    tile = scores.shape[2]
    rows = q_lat.shape[0]
    top[...] = jnp.full_like(top, very_negative)
    total[...] = jnp.zeros_like(total)
    weighted[...] = jnp.zeros_like(weighted)

    def score(i):
        k = pref[pl.ds(2 * i, 2)].reshape(tile, width)
        s = contract_last(q_out[...].reshape(rows, width), k) * score_scale
        scores[i] = s
        top[...] = jnp.maximum(top[...], jnp.max(s, axis=1, keepdims=True))

    def attend_at(hop):
        if hop == ATTEND_AFTER:
            queries.finish()
            loop(owned, attend_and_send)

    arrived(other)
    send_on(other, 0, up)
    send_on(other, 1, down)
    attend_at(0)
    for hop in (1, 2, 3):
        for column in (0, 1):
            c = shard_of(-hop, column)
            arrived(c)
            if hop < 3 or column == 0:
                send_on(c, 0, up)
            c = shard_of(hop, column)
            arrived(c)
            if hop < 3 or column == 1:
                send_on(c, 1, down)
        attend_at(hop)
    for column in (0, 1):
        arrived(shard_of(4, column))
    loop(half, score)

    def weigh(i):
        e = jnp.exp(scores[i] - top[...])
        total[...] += jnp.sum(e, axis=1, keepdims=True)
        k = pref[pl.ds(2 * i, 2), :, pl.ds(0, latent)].reshape(tile, latent)
        weighted[...] += jnp.dot(e.astype(jnp.bfloat16), k, preferred_element_type=jnp.float32)

    loop(half, weigh)

    def merge(a, j):
        at = pl.ds(pl.multiple_of(j * own_rows + a * block, block), block)
        tail = part_in[a, j, :, pl.ds(latent, lanes)].astype(jnp.float32)
        lse = jnp.sum(tail, axis=1, keepdims=True)
        part = part_in[a, j, :, pl.ds(0, latent)].astype(jnp.float32)
        m = jnp.maximum(top[at], lse)
        scale, part_scale = jnp.exp(top[at] - m), jnp.exp(lse - m)
        share = 1.0 / (total[at] * scale + part_scale)
        out[at] = (weighted[at] * (scale * share) + part * (part_scale * share)).astype(jnp.bfloat16)

    def merge_all(a):
        part_exchange(a).finish()

        def four(i):
            for j in range(4):
                merge(a, 4 * i + j)

        loop(members // 4, four)

    loop(owned, merge_all)
    for exchange in [one, two, pages, queries] + [f(a) for a in range(owned) for f in (key_exchange, part_exchange)]:
        exchange.drain()
    for c, way, where in sends:
        ring(c, way, where).wait_send()


def attention(members, q_lat, q_rope, new_latent, prefix_shard, store_order, prefix_of_group, private_store, request_source, private_len):
    groups, capacity, depth, width = private_store.shape
    rows, latent = q_lat.shape
    rope = q_rope.shape[1]
    requests = new_latent.shape[0]
    owned = requests // members
    own = rows // members
    shard = prefix_shard.shape[0]
    lanes = latent // 4
    wide = latent + lanes
    bf16, f32 = jnp.bfloat16, jnp.float32
    vmem, smem, anywhere = [pl.BlockSpec(memory_space=m) for m in (pltpu.VMEM, pltpu.SMEM, pl.ANY)]
    dma = pltpu.SemaphoreType.DMA
    return pl.pallas_call(
        functools.partial(kernel, groups, members),
        out_shape=jax.ShapeDtypeStruct((rows, latent), bf16),
        in_specs=[vmem, vmem, vmem, vmem, vmem, smem, smem, anywhere, smem, smem],
        out_specs=vmem,
        scratch_shapes=[pltpu.VMEM((members, own, wide), bf16)] * 2
        + [pltpu.VMEM((groups, 32, lanes), bf16)] * 4
        + [
            pltpu.VMEM((members, shard, wide), bf16),
            pltpu.VMEM((members // 2, rows, 2 * shard), f32),
            pltpu.VMEM((rows, latent), f32),
            pltpu.VMEM((rows, 1), f32),
            pltpu.VMEM((rows, 1), f32),
            pltpu.VMEM((groups, capacity, depth, width), bf16),
            pltpu.VMEM((requests, depth, width), bf16),
            pltpu.VMEM((owned, members, depth, width), bf16),
            pltpu.VMEM((owned, members, own // owned, wide), bf16),
            pltpu.VMEM((owned, members, own // owned, wide), bf16),
            pltpu.SMEM((requests,), jnp.int32),
        ]
        + [dma((groups,))] * 4
        + [dma((3, members)), dma((members,))]
        + [dma((groups,))] * 2
        + [dma((owned, members))] * 2
        + [dma((members,))] * 2
        + [dma((owned, members))] * 2,
        compiler_params=pltpu.CompilerParams(collective_id=0, has_side_effects=True, vmem_limit_bytes=40 * MIB),
        cost_estimate=pl.CostEstimate(flops=2_700_000_000, bytes_accessed=8_000_000, transcendentals=2_000_000),
    )(
        q_lat,
        q_rope,
        new_latent,
        prefix_shard[:, :latent],
        prefix_shard[:, latent:],
        store_order,
        prefix_of_group,
        private_store,
        request_source,
        private_len,
    )


def shards(
    members,
    q_nope,
    q_rope,
    new_latent,
    w_uk,
    w_uv,
    prefix_store,
    store_order,
    prefix_of_group,
    private_store,
    request_source,
    private_len,
):
    requests, steps, heads = q_nope.shape[:3]
    rows = requests * steps * heads
    q_lat = jnp.einsum("rthn,hnc->rthc", q_nope, w_uk, preferred_element_type=jnp.float32).astype(jnp.bfloat16)
    q_lat, q_rope = q_lat.reshape(rows, -1), q_rope.reshape(rows, -1)
    attended = attention(
        members,
        q_lat,
        q_rope,
        new_latent,
        prefix_store[0],
        store_order,
        prefix_of_group,
        private_store[0],
        request_source[:, 0],
        private_len[0],
    )
    attended = attended.reshape(requests, steps, heads, -1)
    return jnp.einsum("rthc,hcv->rthv", attended, w_uv, preferred_element_type=jnp.float32).astype(jnp.bfloat16)


def solution(mesh):
    in_specs = (
        P("rep", None, "grp", None),
        P("rep", None, "grp", None),
        P("rep", None, None),
        P("grp", None, None),
        P("grp", None, None),
        P("rep", "grp", None),
        P(),
        P(),
        P("rep", None, None, "grp", None),
        P("rep", None),
        P("rep", None),
    )
    out_specs = P("rep", None, "grp", None)
    body = functools.partial(shards, mesh.shape["grp"])
    return jax.shard_map(body, mesh=mesh, in_specs=in_specs, out_specs=out_specs, check_vma=False)
```

```python
import functools

import jax
import jax.numpy as jnp
from jax import lax
from jax.experimental import pallas as pl
from jax.experimental.pallas import tpu as pltpu
from jax.sharding import PartitionSpec as P

score_scale = 192.0 ** (-0.5)
very_negative = -1e30
MIB = 1024 * 1024
MESH = pl.DeviceIdType.MESH
EARLY = 12
ODD_PAGES = 1


def contract_last(a, b):
    return lax.dot_general(a, b, (((1,), (1,)), ((), ())), preferred_element_type=jnp.float32)


def loop(count, body):
    def step(i, carry):
        body(i)
        return carry

    lax.fori_loop(0, count, step, 0)


def remote(src, dst, send, recv, where):
    return pltpu.make_async_remote_copy(
        src_ref=src, dst_ref=dst, send_sem=send, recv_sem=recv, device_id=where, device_id_type=MESH
    )


def greet(groups, members):
    me, mine = lax.axis_index("rep"), lax.axis_index("grp")
    barrier = pltpu.get_barrier_semaphore()

    def along_rep(k):
        pl.semaphore_signal(barrier, inc=1, device_id={"rep": (me + k + 1) % groups}, device_id_type=MESH)

    def along_grp(k):
        pl.semaphore_signal(barrier, inc=1, device_id={"grp": (mine + k + 1) % members}, device_id_type=MESH)

    loop(groups - 1, along_rep)
    loop(members - 1, along_grp)
    pl.semaphore_wait(barrier, groups + members - 2)


class Exchange:
    def __init__(self, axis, peers, out_ref, in_ref, send, recv):
        self.axis, self.peers, self.out_ref, self.in_ref, self.send, self.recv = axis, peers, out_ref, in_ref, send, recv
        self.me = lax.axis_index(axis)

    def peer(self, k):
        return (self.me + k + 1) % self.peers

    def to(self, j):
        return remote(self.out_ref(j), self.in_ref(self.me), self.send(j), self.recv(self.me), {self.axis: j})

    def own(self):
        return pltpu.make_async_copy(self.out_ref(self.me), self.in_ref(self.me), self.recv(self.me))

    def start(self, begin=0, end=None):
        loop((self.peers - 1 if end is None else end) - begin, lambda k: self.to(self.peer(k + begin)).start())

    def arrive(self, j):
        remote(self.out_ref(j), self.in_ref(j), self.send(j), self.recv(j), {self.axis: j}).wait_recv()

    def finish(self):
        self.own().wait()
        loop(self.peers - 1, lambda k: self.arrive(self.peer(k)))

    def drain(self):
        loop(self.peers - 1, lambda k: self.to(self.peer(k)).wait_send())


def kernel(
    groups,
    members,
    q_lat,
    q_rope,
    new_latent,
    prefix_shard,
    store_order,
    prefix_of_group,
    private_store,
    request_source,
    private_len,
    out,
    q_out,
    q_in,
    one_out,
    one_in,
    two_out,
    two_in,
    pref,
    scores,
    weighted,
    top,
    total,
    pages_in,
    pages_out0,
    pages_out1,
    keys0,
    keys1,
    part_out0,
    part_out1,
    part_in0,
    part_in1,
    slots,
    one_send,
    one_recv,
    two_send,
    two_recv,
    ring_send,
    ring_recv,
    pages_send,
    pages_recv,
    keys_send,
    keys_recv,
    q_send,
    q_recv,
    part_send,
    part_recv,
):
    me, mine = lax.axis_index("rep"), lax.axis_index("grp")
    half = members // 2
    z, y = mine // 2, mine % 2
    latent, rope = q_lat.shape[1], q_rope.shape[1]
    lanes = latent // 4
    requests = request_source.shape[0]
    owned = requests // members
    capacity, depth = private_store.shape[1:3]
    own_rows = q_lat.shape[0] // members
    block = own_rows // owned
    shard = prefix_shard.shape[0]

    def rows_of(j):
        return pl.ds(pl.multiple_of((j // 4) * 16, 16), 16)

    def columns_of(j):
        return pl.ds(pl.multiple_of((j % 4) * lanes, lanes), lanes)

    def cut(j):
        one_out[j, pl.ds(0, 16)] = prefix_shard[rows_of(j), columns_of(j)]

    def cut_rope(j):
        sides = [prefix_shard[pl.ds(pl.multiple_of((j % 4) * 32 + 16 * side, 16), 16), pl.ds(latent, rope)] for side in (0, 1)]
        one_out[j, pl.ds(16, 16)] = jnp.concatenate(sides, axis=1)

    loop(groups, cut)
    loop(groups, cut_rope)

    def query_rows(j):
        return pl.ds(pl.multiple_of(j * own_rows, own_rows), own_rows)

    def put_query(j):
        q_out[j, :, pl.ds(0, latent)] = q_lat[query_rows(j)]
        q_out[j, :, pl.ds(latent, lanes)] = jnp.concatenate(
            [q_rope[query_rows(j)], jnp.zeros((own_rows, lanes - rope), jnp.bfloat16)], axis=1
        )

    loop(members, put_query)
    greet(groups, members)
    one = Exchange("rep", groups, lambda j: one_out.at[j], lambda j: one_in.at[j], lambda j: one_send.at[j], lambda j: one_recv.at[j])
    two = Exchange("rep", groups, lambda j: two_out.at[j], lambda j: two_in.at[j], lambda j: two_send.at[j], lambda j: two_recv.at[j])
    pages = Exchange("rep", groups, lambda j: private_store.at[j], lambda j: pages_in.at[j], lambda j: pages_send.at[j], lambda j: pages_recv.at[j])
    queries = Exchange("grp", members, lambda j: q_out.at[j], lambda j: q_in.at[j], lambda j: q_send.at[j], lambda j: q_recv.at[j])

    def exchange_of(a, outs, ins, send, recv):
        return Exchange("grp", members, lambda j: outs[a].at[j], lambda j: ins[a].at[j], lambda j: send.at[a, j], lambda j: recv.at[a, j])

    def key_exchange(a):
        return exchange_of(a, (pages_out0, pages_out1), (keys0, keys1), keys_send, keys_recv)

    def part_exchange(a):
        return exchange_of(a, (part_out0, part_out1), (part_in0, part_in1), part_send, part_recv)

    one.start()
    one.own().start()

    @pl.when(me % 2 == 1)
    def _():
        queries.start()

    @pl.when(me % 2 == 0)
    def _():
        pages.start(0, EARLY)

    pages.own().start()
    queries.own().start()
    one.finish()

    def choose(j):
        two_out[j] = one_in[store_order[prefix_of_group[j]]]

    loop(groups, choose)
    two.start()
    two.own().start()

    @pl.when(me % 2 == 0)
    def _():
        pages.start(EARLY, groups - 1)

        queries.start()

    def find_slot(i):
        source = request_source[i]

        def count(j, rank):
            return rank + jnp.where((request_source[j] == source) & (j < i), 1, 0)

        slots[i] = jnp.minimum(lax.fori_loop(0, requests, count, jnp.int32(0)), capacity - 1)

    loop(requests, find_slot)
    two.finish()

    def place(j):
        pref[mine, rows_of(j), columns_of(j)] = two_in[j, pl.ds(0, 16)]

    def place_rope(j):
        pref[mine, pl.ds(shard, 16), columns_of(j)] = two_in[j, pl.ds(16, 16)]

    loop(groups, place)
    loop(4, place_rope)

    across = {"grp": z * 2 + 1 - y}
    up, down = {"grp": ((z + 1) % half) * 2 + y}, {"grp": ((z + half - 1) % half) * 2 + y}

    def shard_of(dz, column):
        return ((z + dz + half) % half) * 2 + column

    def ring(c, way, where):
        return remote(pref.at[c], pref.at[c], ring_send.at[way, c], ring_recv.at[c], where)

    def arrived(c):
        ring(c, 0, up).wait_recv()

    sends = []

    def send_on(c, way, where):
        ring(c, way, where).start()
        sends.append((c, way, where))

    other = shard_of(0, 1 - y)
    send_on(mine, 0, up)
    send_on(mine, 1, down)
    send_on(mine, 2, across)
    def attend(a, earlier):
        rows = members * block
        q = q_in[:, pl.ds(a * block, block), :].reshape(rows, latent + lanes)[:, : latent + rope]
        k_lat = (keys0[:, :, pl.ds(0, latent)], keys1[...])[a].reshape(members * depth, latent)
        k_rope = keys0[:, :, pl.ds(latent, lanes)].reshape(members * depth, lanes)[:, rope * a : rope * (a + 1)]
        s = (contract_last(q[:, :latent], k_lat) + contract_last(q[:, latent:], k_rope)) * score_scale
        usable = lax.broadcasted_iota(jnp.int32, s.shape, 1) < private_len[mine * owned + a]
        s = jnp.where(usable, s, very_negative)
        fresh = new_latent[mine * owned + a].astype(jnp.float32)
        q32 = q.astype(jnp.float32)
        step = (lax.broadcasted_iota(jnp.int32, (rows, 1), 0) % block) // (block // 2)
        new_s = []
        for u in range(2):
            s_u = jnp.sum(q32 * fresh[u : u + 1], axis=1, keepdims=True) * score_scale
            new_s.append(jnp.where(step >= u, s_u, very_negative))
        m = jnp.maximum(jnp.max(s, axis=1, keepdims=True), jnp.maximum(new_s[0], new_s[1]))
        e = jnp.where(usable, jnp.exp(s - m), 0.0)
        length = jnp.sum(e, axis=1, keepdims=True)
        summed = jnp.dot(e.astype(jnp.bfloat16), k_lat, preferred_element_type=jnp.float32)
        for u in range(2):
            e_u = jnp.where(step >= u, jnp.exp(new_s[u] - m), 0.0)
            length = length + e_u
            summed = summed + e_u.astype(jnp.bfloat16).astype(jnp.float32) * fresh[u : u + 1, :latent]
        lse = m + jnp.log(length)
        high = lse.astype(jnp.bfloat16).astype(jnp.float32)
        middle = (lse - high).astype(jnp.bfloat16).astype(jnp.float32)
        low = lse - high - middle
        place = lax.broadcasted_iota(jnp.int32, (rows, lanes), 1)
        tail = jnp.where(place == 3 * a, high, jnp.where(place == 3 * a + 1, middle, jnp.where(place == 3 * a + 2, low, earlier)))
        (part_out0, part_out1)[a][:, :, pl.ds(0, latent)] = (summed / length).astype(jnp.bfloat16).reshape(members, block, latent)
        if a == 1:
            part_out1[:, :, pl.ds(latent, lanes)] = tail.astype(jnp.bfloat16).reshape(members, block, lanes)
        return tail

    def attend_both():
        tail = 0.0
        for a in range(2):
            key_exchange(a).finish()
            tail = attend(a, tail)
            part_exchange(a).start()
            part_exchange(a).own().start()

    tile = scores.shape[2]
    rows = q_lat.shape[0]
    top[...] = jnp.full_like(top, very_negative)
    total[...] = jnp.zeros_like(total)
    weighted[...] = jnp.zeros_like(weighted)

    def odd_pages(hop):
        if hop == ODD_PAGES:

            @pl.when(me % 2 == 1)
            def _():
                pages.start()

    arrived(other)
    send_on(other, 0, up)
    send_on(other, 1, down)
    odd_pages(0)
    for hop in (1, 2, 3):
        for column in (0, 1):
            c = shard_of(-hop, column)
            arrived(c)
            if hop < 3 or column == 0:
                send_on(c, 0, up)
            c = shard_of(hop, column)
            arrived(c)
            if hop < 3 or column == 1:
                send_on(c, 1, down)
        odd_pages(hop)
    for column in (0, 1):
        arrived(shard_of(4, column))

    def score(i):
        k_lat = pref[pl.ds(2 * i, 2), pl.ds(0, shard)].reshape(tile, latent)
        packed = [pref[2 * i + n, pl.ds(shard, 16)] for n in range(2)]
        k_rope = jnp.concatenate([p[:, rope * b : rope * (b + 1)] for p in packed for b in range(shard // 16)], axis=0)
        q = q_out[...].reshape(rows, latent + lanes)
        s = (contract_last(q[:, :latent], k_lat) + contract_last(q[:, latent : latent + rope], k_rope)) * score_scale
        scores[i] = s
        top[...] = jnp.maximum(top[...], jnp.max(s, axis=1, keepdims=True))

    pages.finish()

    def pick(j):
        first, second = [pages_in[request_source[2 * j + a], slots[2 * j + a]] for a in range(2)]
        pages_out0[j, :, pl.ds(0, latent)] = first[:, :latent]
        pages_out0[j, :, pl.ds(latent, lanes)] = jnp.concatenate([first[:, latent:], second[:, latent:]], axis=1)
        pages_out1[j] = second[:, :latent]

    loop(members, pick)
    for a in range(2):
        key_exchange(a).start()
        key_exchange(a).own().start()

    loop(half, score)

    def weigh(i):
        e = jnp.exp(scores[i] - top[...])
        total[...] += jnp.sum(e, axis=1, keepdims=True)
        k = pref[pl.ds(2 * i, 2), pl.ds(0, shard)].reshape(tile, latent)
        weighted[...] += jnp.dot(e.astype(jnp.bfloat16), k, preferred_element_type=jnp.float32)

    loop(half, weigh)
    queries.finish()
    attend_both()

    def merge(a, j):
        at = pl.ds(pl.multiple_of(j * own_rows + a * block, block), block)
        tail = part_in1[j, :, pl.ds(latent, lanes)].astype(jnp.float32)
        mine_of_tail = lax.broadcasted_iota(jnp.int32, tail.shape, 1) // 3 == a
        lse = jnp.sum(jnp.where(mine_of_tail, tail, 0.0), axis=1, keepdims=True)
        part = (part_in0[j], part_in1[j, :, pl.ds(0, latent)])[a].astype(jnp.float32)
        m = jnp.maximum(top[at], lse)
        scale, part_scale = jnp.exp(top[at] - m), jnp.exp(lse - m)
        share = 1.0 / (total[at] * scale + part_scale)
        out[at] = (weighted[at] * (scale * share) + part * (part_scale * share)).astype(jnp.bfloat16)

    part_exchange(0).finish()
    part_exchange(1).finish()

    def merge_two(i):
        for j in range(2):
            for a in range(2):
                merge(a, 2 * i + j)

    loop(members // 2, merge_two)
    for exchange in [one, two, pages, queries] + [f(a) for a in range(owned) for f in (key_exchange, part_exchange)]:
        exchange.drain()
    for c, way, where in sends:
        ring(c, way, where).wait_send()


def attention(members, q_lat, q_rope, new_latent, prefix_shard, store_order, prefix_of_group, private_store, request_source, private_len):
    groups, capacity, depth, width = private_store.shape
    rows, latent = q_lat.shape
    rope = q_rope.shape[1]
    requests = new_latent.shape[0]
    owned = requests // members
    own = rows // members
    shard = prefix_shard.shape[0]
    lanes = latent // 4
    wide = latent + lanes
    bf16, f32 = jnp.bfloat16, jnp.float32
    vmem, smem, anywhere = [pl.BlockSpec(memory_space=m) for m in (pltpu.VMEM, pltpu.SMEM, pl.ANY)]
    dma = pltpu.SemaphoreType.DMA
    return pl.pallas_call(
        functools.partial(kernel, groups, members),
        out_shape=jax.ShapeDtypeStruct((rows, latent), bf16),
        in_specs=[vmem, vmem, vmem, vmem, smem, smem, anywhere, smem, smem],
        out_specs=vmem,
        scratch_shapes=[pltpu.VMEM((members, own, wide), bf16)] * 2
        + [pltpu.VMEM((groups, 32, lanes), bf16)] * 4
        + [
            pltpu.VMEM((members, shard + 16, latent), bf16),
            pltpu.VMEM((members // 2, rows, 2 * shard), f32),
            pltpu.VMEM((rows, latent), f32),
            pltpu.VMEM((rows, 1), f32),
            pltpu.VMEM((rows, 1), f32),
            pltpu.VMEM((groups, capacity, depth, width), bf16),
        ]
        + [pltpu.VMEM((members, depth, w), bf16) for w in (wide, latent)] * 2
        + [pltpu.VMEM((members, own // owned, w), bf16) for w in (latent, wide)] * 2
        + [
            pltpu.SMEM((requests,), jnp.int32),
        ]
        + [dma((groups,))] * 4
        + [dma((3, members)), dma((members,))]
        + [dma((groups,))] * 2
        + [dma((owned, members))] * 2
        + [dma((members,))] * 2
        + [dma((owned, members))] * 2,
        compiler_params=pltpu.CompilerParams(collective_id=0, has_side_effects=True, vmem_limit_bytes=24 * MIB),
        cost_estimate=pl.CostEstimate(flops=2_700_000_000, bytes_accessed=8_000_000, transcendentals=2_000_000),
    )(
        q_lat,
        q_rope,
        new_latent,
        prefix_shard,
        store_order,
        prefix_of_group,
        private_store,
        request_source,
        private_len,
    )


def shards(
    members,
    q_nope,
    q_rope,
    new_latent,
    w_uk,
    w_uv,
    prefix_store,
    store_order,
    prefix_of_group,
    private_store,
    request_source,
    private_len,
):
    requests, steps, heads = q_nope.shape[:3]
    rows = requests * steps * heads
    q_lat = jnp.einsum("rthn,hnc->rthc", q_nope, w_uk, preferred_element_type=jnp.float32).astype(jnp.bfloat16)
    q_lat, q_rope = q_lat.reshape(rows, -1), q_rope.reshape(rows, -1)
    attended = attention(
        members,
        q_lat,
        q_rope,
        new_latent,
        prefix_store[0],
        store_order,
        prefix_of_group,
        private_store[0],
        request_source[:, 0],
        private_len[0],
    )
    attended = attended.reshape(requests, steps, heads, -1)
    return jnp.einsum("rthc,hcv->rthv", attended, w_uv, preferred_element_type=jnp.float32).astype(jnp.bfloat16)


def solution(mesh):
    in_specs = (
        P("rep", None, "grp", None),
        P("rep", None, "grp", None),
        P("rep", None, None),
        P("grp", None, None),
        P("grp", None, None),
        P("rep", "grp", None),
        P(),
        P(),
        P("rep", None, None, "grp", None),
        P("rep", None),
        P("rep", None),
    )
    out_specs = P("rep", None, "grp", None)
    body = functools.partial(shards, mesh.shape["grp"])
    return jax.shard_map(body, mesh=mesh, in_specs=in_specs, out_specs=out_specs, check_vma=False)
```

```python
import functools

import jax
import jax.numpy as jnp
from jax import lax
from jax.experimental import pallas as pl
from jax.experimental.pallas import tpu as pltpu
from jax.sharding import PartitionSpec as P

score_scale = 192.0 ** (-0.5)
very_negative = -1e30
MIB = 1024 * 1024
MESH = pl.DeviceIdType.MESH
EARLY = 16
ODD_PAGES = 1
PICK_AFTER = 3


def contract_last(a, b):
    return lax.dot_general(a, b, (((1,), (1,)), ((), ())), preferred_element_type=jnp.float32)


def loop(count, body):
    def step(i, carry):
        body(i)
        return carry

    lax.fori_loop(0, count, step, 0)


def remote(src, dst, send, recv, where):
    return pltpu.make_async_remote_copy(
        src_ref=src, dst_ref=dst, send_sem=send, recv_sem=recv, device_id=where, device_id_type=MESH
    )


def greet(groups, members):
    me, mine = lax.axis_index("rep"), lax.axis_index("grp")
    barrier = pltpu.get_barrier_semaphore()

    def along_rep(k):
        pl.semaphore_signal(barrier, inc=1, device_id={"rep": (me + k + 1) % groups}, device_id_type=MESH)

    def along_grp(k):
        pl.semaphore_signal(barrier, inc=1, device_id={"grp": (mine + k + 1) % members}, device_id_type=MESH)

    loop(groups - 1, along_rep)
    loop(members - 1, along_grp)
    pl.semaphore_wait(barrier, groups + members - 2)


class Exchange:
    def __init__(self, axis, peers, out_ref, in_ref, send, recv):
        self.axis, self.peers, self.out_ref, self.in_ref, self.send, self.recv = axis, peers, out_ref, in_ref, send, recv
        self.me = lax.axis_index(axis)

    def peer(self, k):
        away = (k // 2 + 1) * (1 - 2 * (k % 2)) if self.axis == "grp" else k + 1
        return (self.me + self.peers + away) % self.peers

    def to(self, j):
        return remote(self.out_ref(j), self.in_ref(self.me), self.send(j), self.recv(self.me), {self.axis: j})

    def own(self):
        return pltpu.make_async_copy(self.out_ref(self.me), self.in_ref(self.me), self.recv(self.me))

    def start(self, begin=0, end=None):
        loop((self.peers - 1 if end is None else end) - begin, lambda k: self.to(self.peer(k + begin)).start())

    def arrive(self, j):
        remote(self.out_ref(j), self.in_ref(j), self.send(j), self.recv(j), {self.axis: j}).wait_recv()

    def finish(self):
        self.own().wait()
        loop(self.peers - 1, lambda k: self.arrive(self.peer(k)))

    def drain(self):
        loop(self.peers - 1, lambda k: self.to(self.peer(k)).wait_send())


def kernel(
    groups,
    members,
    q_lat,
    q_rope,
    new_latent,
    prefix_shard,
    store_order,
    prefix_of_group,
    private_store,
    request_source,
    private_len,
    out,
    q_out,
    q_in,
    one_out,
    one_in,
    two_out,
    two_in,
    pref,
    scores,
    weighted,
    top,
    total,
    pages_in,
    pages_out0,
    pages_out1,
    keys0,
    keys1,
    part_out0,
    part_out1,
    part_in0,
    part_in1,
    slots,
    one_send,
    one_recv,
    two_send,
    two_recv,
    ring_send,
    ring_recv,
    pages_send,
    pages_recv,
    keys_send,
    keys_recv,
    q_send,
    q_recv,
    part_send,
    part_recv,
):
    me, mine = lax.axis_index("rep"), lax.axis_index("grp")
    half = members // 2
    z, y = mine // 2, mine % 2
    latent, rope = q_lat.shape[1], q_rope.shape[1]
    lanes = latent // 4
    requests = request_source.shape[0]
    owned = requests // members
    capacity, depth = private_store.shape[1:3]
    own_rows = q_lat.shape[0] // members
    block = own_rows // owned
    shard = prefix_shard.shape[0]

    def rows_of(j):
        return pl.ds(pl.multiple_of((j // 4) * 16, 16), 16)

    def columns_of(j):
        return pl.ds(pl.multiple_of((j % 4) * lanes, lanes), lanes)

    def cut(j):
        one_out[j, pl.ds(0, 16)] = prefix_shard[rows_of(j), columns_of(j)]

    def cut_rope(j):
        sides = [prefix_shard[pl.ds(pl.multiple_of((j % 4) * 32 + 16 * side, 16), 16), pl.ds(latent, rope)] for side in (0, 1)]
        one_out[j, pl.ds(16, 16)] = jnp.concatenate(sides, axis=1)

    loop(groups, cut)
    loop(groups, cut_rope)

    def query_rows(j):
        return pl.ds(pl.multiple_of(j * own_rows, own_rows), own_rows)

    def put_query(j):
        q_out[j, :, pl.ds(0, latent)] = q_lat[query_rows(j)]
        q_out[j, :, pl.ds(latent, lanes)] = jnp.concatenate(
            [q_rope[query_rows(j)], jnp.zeros((own_rows, lanes - rope), jnp.bfloat16)], axis=1
        )

    loop(members, put_query)
    greet(groups, members)
    one = Exchange("rep", groups, lambda j: one_out.at[j], lambda j: one_in.at[j], lambda j: one_send.at[j], lambda j: one_recv.at[j])
    two = Exchange("rep", groups, lambda j: two_out.at[j], lambda j: two_in.at[j], lambda j: two_send.at[j], lambda j: two_recv.at[j])
    pages = Exchange("rep", groups, lambda j: private_store.at[j], lambda j: pages_in.at[j], lambda j: pages_send.at[j], lambda j: pages_recv.at[j])
    queries = Exchange("grp", members, lambda j: q_out.at[j], lambda j: q_in.at[j], lambda j: q_send.at[j], lambda j: q_recv.at[j])

    def exchange_of(a, outs, ins, send, recv):
        return Exchange("grp", members, lambda j: outs[a].at[j], lambda j: ins[a].at[j], lambda j: send.at[a, j], lambda j: recv.at[a, j])

    def key_exchange(a):
        return exchange_of(a, (pages_out0, pages_out1), (keys0, keys1), keys_send, keys_recv)

    def part_exchange(a):
        return exchange_of(a, (part_out0, part_out1), (part_in0, part_in1), part_send, part_recv)

    one.start()
    one.own().start()

    @pl.when(me % 2 == 1)
    def _():
        queries.start()

    @pl.when(me % 2 == 0)
    def _():
        pages.start(0, EARLY)

    pages.own().start()
    queries.own().start()
    one.finish()

    def choose(j):
        two_out[j] = one_in[store_order[prefix_of_group[j]]]

    loop(groups, choose)
    two.start()
    two.own().start()

    @pl.when(me % 2 == 0)
    def _():
        pages.start(EARLY, groups - 1)

        queries.start()

    def find_slot(i):
        source = request_source[i]

        def count(j, rank):
            return rank + jnp.where((request_source[j] == source) & (j < i), 1, 0)

        slots[i] = jnp.minimum(lax.fori_loop(0, requests, count, jnp.int32(0)), capacity - 1)

    loop(requests, find_slot)
    two.finish()

    def place(j):
        pref[mine, rows_of(j), columns_of(j)] = two_in[j, pl.ds(0, 16)]

    def place_rope(j):
        pref[mine, pl.ds(shard, 16), columns_of(j)] = two_in[j, pl.ds(16, 16)]

    loop(groups, place)
    loop(4, place_rope)

    across = {"grp": z * 2 + 1 - y}
    up, down = {"grp": ((z + 1) % half) * 2 + y}, {"grp": ((z + half - 1) % half) * 2 + y}

    def shard_of(dz, column):
        return ((z + dz + half) % half) * 2 + column

    def ring(c, way, where):
        return remote(pref.at[c], pref.at[c], ring_send.at[way, c], ring_recv.at[c], where)

    def arrived(c):
        ring(c, 0, up).wait_recv()

    sends = []

    def send_on(c, way, where):
        ring(c, way, where).start()
        sends.append((c, way, where))

    other = shard_of(0, 1 - y)
    send_on(mine, 0, up)
    send_on(mine, 1, down)
    send_on(mine, 2, across)
    def attend(a, earlier):
        rows = members * block
        q = q_in[:, pl.ds(a * block, block), :].reshape(rows, latent + lanes)[:, : latent + rope]
        k_lat = (keys0[:, :, pl.ds(0, latent)], keys1[...])[a].reshape(members * depth, latent)
        k_rope = keys0[:, :, pl.ds(latent, lanes)].reshape(members * depth, lanes)[:, rope * a : rope * (a + 1)]
        s = (contract_last(q[:, :latent], k_lat) + contract_last(q[:, latent:], k_rope)) * score_scale
        usable = lax.broadcasted_iota(jnp.int32, s.shape, 1) < private_len[mine * owned + a]
        s = jnp.where(usable, s, very_negative)
        fresh = new_latent[mine * owned + a].astype(jnp.float32)
        q32 = q.astype(jnp.float32)
        step = (lax.broadcasted_iota(jnp.int32, (rows, 1), 0) % block) // (block // 2)
        new_s = []
        for u in range(2):
            s_u = jnp.sum(q32 * fresh[u : u + 1], axis=1, keepdims=True) * score_scale
            new_s.append(jnp.where(step >= u, s_u, very_negative))
        m = jnp.maximum(jnp.max(s, axis=1, keepdims=True), jnp.maximum(new_s[0], new_s[1]))
        e = jnp.where(usable, jnp.exp(s - m), 0.0)
        length = jnp.sum(e, axis=1, keepdims=True)
        summed = jnp.dot(e.astype(jnp.bfloat16), k_lat, preferred_element_type=jnp.float32)
        for u in range(2):
            e_u = jnp.where(step >= u, jnp.exp(new_s[u] - m), 0.0)
            length = length + e_u
            summed = summed + e_u.astype(jnp.bfloat16).astype(jnp.float32) * fresh[u : u + 1, :latent]
        lse = m + jnp.log(length)
        high = lse.astype(jnp.bfloat16).astype(jnp.float32)
        middle = (lse - high).astype(jnp.bfloat16).astype(jnp.float32)
        low = lse - high - middle
        place = lax.broadcasted_iota(jnp.int32, (rows, lanes), 1)
        tail = jnp.where(place == 3 * a, high, jnp.where(place == 3 * a + 1, middle, jnp.where(place == 3 * a + 2, low, earlier)))
        (part_out0, part_out1)[a][:, :, pl.ds(0, latent)] = (summed / length).astype(jnp.bfloat16).reshape(members, block, latent)
        if a == 1:
            part_out1[:, :, pl.ds(latent, lanes)] = tail.astype(jnp.bfloat16).reshape(members, block, lanes)
        return tail

    def attend_both():
        tail = 0.0
        for a in range(2):
            key_exchange(a).finish()
            tail = attend(a, tail)
            part_exchange(a).start()
            part_exchange(a).own().start()

    tile = scores.shape[2]
    rows = q_lat.shape[0]
    top[...] = jnp.full_like(top, very_negative)
    total[...] = jnp.zeros_like(total)
    weighted[...] = jnp.zeros_like(weighted)

    def odd_pages(hop):
        if hop == ODD_PAGES:

            @pl.when(me % 2 == 1)
            def _():
                pages.start()

    def send_keys():
        pages.finish()

        def pick(j):
            first, second = [pages_in[request_source[2 * j + a], slots[2 * j + a]] for a in range(2)]
            pages_out0[j, :, pl.ds(0, latent)] = first[:, :latent]
            pages_out0[j, :, pl.ds(latent, lanes)] = jnp.concatenate([first[:, latent:], second[:, latent:]], axis=1)
            pages_out1[j] = second[:, :latent]

        loop(members, pick)
        for a in range(2):
            key_exchange(a).start()
            key_exchange(a).own().start()

    arrived(other)
    send_on(other, 0, up)
    send_on(other, 1, down)
    odd_pages(0)
    for hop in (1, 2, 3):
        for column in (0, 1):
            c = shard_of(-hop, column)
            arrived(c)
            if hop < 3 or column == 0:
                send_on(c, 0, up)
            c = shard_of(hop, column)
            arrived(c)
            if hop < 3 or column == 1:
                send_on(c, 1, down)
        odd_pages(hop)
        if hop == PICK_AFTER:
            send_keys()
    for column in (0, 1):
        arrived(shard_of(4, column))

    def score(i):
        k_lat = pref[pl.ds(2 * i, 2), pl.ds(0, shard)].reshape(tile, latent)
        packed = [pref[2 * i + n, pl.ds(shard, 16)] for n in range(2)]
        k_rope = jnp.concatenate([p[:, rope * b : rope * (b + 1)] for p in packed for b in range(shard // 16)], axis=0)
        q = q_out[...].reshape(rows, latent + lanes)
        s = (contract_last(q[:, :latent], k_lat) + contract_last(q[:, latent : latent + rope], k_rope)) * score_scale
        scores[i] = s
        top[...] = jnp.maximum(top[...], jnp.max(s, axis=1, keepdims=True))

    loop(half, score)

    def weigh(i):
        e = jnp.exp(scores[i] - top[...])
        total[...] += jnp.sum(e, axis=1, keepdims=True)
        k = pref[pl.ds(2 * i, 2), pl.ds(0, shard)].reshape(tile, latent)
        weighted[...] += jnp.dot(e.astype(jnp.bfloat16), k, preferred_element_type=jnp.float32)

    loop(half, weigh)
    queries.finish()
    attend_both()

    def merge(a, j):
        at = pl.ds(pl.multiple_of(j * own_rows + a * block, block), block)
        tail = part_in1[j, :, pl.ds(latent, lanes)].astype(jnp.float32)
        mine_of_tail = lax.broadcasted_iota(jnp.int32, tail.shape, 1) // 3 == a
        lse = jnp.sum(jnp.where(mine_of_tail, tail, 0.0), axis=1, keepdims=True)
        part = (part_in0[j], part_in1[j, :, pl.ds(0, latent)])[a].astype(jnp.float32)
        m = jnp.maximum(top[at], lse)
        scale, part_scale = jnp.exp(top[at] - m), jnp.exp(lse - m)
        share = 1.0 / (total[at] * scale + part_scale)
        out[at] = (weighted[at] * (scale * share) + part * (part_scale * share)).astype(jnp.bfloat16)

    part_exchange(0).finish()
    part_exchange(1).finish()

    def merge_two(i):
        for j in range(2):
            for a in range(2):
                merge(a, 2 * i + j)

    loop(members // 2, merge_two)
    for exchange in [one, two, pages, queries] + [f(a) for a in range(owned) for f in (key_exchange, part_exchange)]:
        exchange.drain()
    for c, way, where in sends:
        ring(c, way, where).wait_send()


def attention(members, q_lat, q_rope, new_latent, prefix_shard, store_order, prefix_of_group, private_store, request_source, private_len):
    groups, capacity, depth, width = private_store.shape
    rows, latent = q_lat.shape
    rope = q_rope.shape[1]
    requests = new_latent.shape[0]
    owned = requests // members
    own = rows // members
    shard = prefix_shard.shape[0]
    lanes = latent // 4
    wide = latent + lanes
    bf16, f32 = jnp.bfloat16, jnp.float32
    vmem, smem, anywhere = [pl.BlockSpec(memory_space=m) for m in (pltpu.VMEM, pltpu.SMEM, pl.ANY)]
    dma = pltpu.SemaphoreType.DMA
    return pl.pallas_call(
        functools.partial(kernel, groups, members),
        out_shape=jax.ShapeDtypeStruct((rows, latent), bf16),
        in_specs=[vmem, vmem, vmem, vmem, smem, smem, anywhere, smem, smem],
        out_specs=vmem,
        scratch_shapes=[pltpu.VMEM((members, own, wide), bf16)] * 2
        + [pltpu.VMEM((groups, 32, lanes), bf16)] * 4
        + [
            pltpu.VMEM((members, shard + 16, latent), bf16),
            pltpu.VMEM((members // 2, rows, 2 * shard), f32),
            pltpu.VMEM((rows, latent), f32),
            pltpu.VMEM((rows, 1), f32),
            pltpu.VMEM((rows, 1), f32),
            pltpu.VMEM((groups, capacity, depth, width), bf16),
        ]
        + [pltpu.VMEM((members, depth, w), bf16) for w in (wide, latent)] * 2
        + [pltpu.VMEM((members, own // owned, w), bf16) for w in (latent, wide)] * 2
        + [
            pltpu.SMEM((requests,), jnp.int32),
        ]
        + [dma((groups,))] * 4
        + [dma((3, members)), dma((members,))]
        + [dma((groups,))] * 2
        + [dma((owned, members))] * 2
        + [dma((members,))] * 2
        + [dma((owned, members))] * 2,
        compiler_params=pltpu.CompilerParams(collective_id=0, has_side_effects=True, vmem_limit_bytes=24 * MIB),
        cost_estimate=pl.CostEstimate(flops=2_700_000_000, bytes_accessed=8_000_000, transcendentals=2_000_000),
    )(
        q_lat,
        q_rope,
        new_latent,
        prefix_shard,
        store_order,
        prefix_of_group,
        private_store,
        request_source,
        private_len,
    )


def shards(
    members,
    q_nope,
    q_rope,
    new_latent,
    w_uk,
    w_uv,
    prefix_store,
    store_order,
    prefix_of_group,
    private_store,
    request_source,
    private_len,
):
    requests, steps, heads = q_nope.shape[:3]
    rows = requests * steps * heads
    q_lat = jnp.einsum("rthn,hnc->rthc", q_nope, w_uk, preferred_element_type=jnp.float32).astype(jnp.bfloat16)
    q_lat, q_rope = q_lat.reshape(rows, -1), q_rope.reshape(rows, -1)
    attended = attention(
        members,
        q_lat,
        q_rope,
        new_latent,
        prefix_store[0],
        store_order,
        prefix_of_group,
        private_store[0],
        request_source[:, 0],
        private_len[0],
    )
    attended = attended.reshape(requests, steps, heads, -1)
    return jnp.einsum("rthc,hcv->rthv", attended, w_uv, preferred_element_type=jnp.float32).astype(jnp.bfloat16)


def solution(mesh):
    in_specs = (
        P("rep", None, "grp", None),
        P("rep", None, "grp", None),
        P("rep", None, None),
        P("grp", None, None),
        P("grp", None, None),
        P("rep", "grp", None),
        P(),
        P(),
        P("rep", None, None, "grp", None),
        P("rep", None),
        P("rep", None),
    )
    out_specs = P("rep", None, "grp", None)
    body = functools.partial(shards, mesh.shape["grp"])
    return jax.shard_map(body, mesh=mesh, in_specs=in_specs, out_specs=out_specs, check_vma=False)
```

```python
import functools

import jax
import jax.numpy as jnp
from jax import lax
from jax.experimental import pallas as pl
from jax.experimental.pallas import tpu as pltpu
from jax.sharding import PartitionSpec as P

score_scale = 192.0 ** (-0.5)
very_negative = -1e30
MIB = 1024 * 1024
MESH = pl.DeviceIdType.MESH
EARLY = 16
ODD_PAGES = 1
PICK_AFTER = 3


def contract_last(a, b):
    return lax.dot_general(a, b, (((1,), (1,)), ((), ())), preferred_element_type=jnp.float32)


def loop(count, body):
    def step(i, carry):
        body(i)
        return carry

    lax.fori_loop(0, count, step, 0)


def remote(src, dst, send, recv, where):
    return pltpu.make_async_remote_copy(
        src_ref=src, dst_ref=dst, send_sem=send, recv_sem=recv, device_id=where, device_id_type=MESH
    )


def greet(groups, members):
    me, mine = lax.axis_index("rep"), lax.axis_index("grp")
    barrier = pltpu.get_barrier_semaphore()

    def along_rep(k):
        pl.semaphore_signal(barrier, inc=1, device_id={"rep": (me + k + 1) % groups}, device_id_type=MESH)

    def along_grp(k):
        pl.semaphore_signal(barrier, inc=1, device_id={"grp": (mine + k + 1) % members}, device_id_type=MESH)

    loop(groups - 1, along_rep)
    loop(members - 1, along_grp)
    pl.semaphore_wait(barrier, groups + members - 2)


class Exchange:
    def __init__(self, axis, peers, out_ref, in_ref, send, recv):
        self.axis, self.peers, self.out_ref, self.in_ref, self.send, self.recv = axis, peers, out_ref, in_ref, send, recv
        self.me = lax.axis_index(axis)

    def peer(self, k):
        away = (k // 2 + 1) * (1 - 2 * (k % 2)) if self.axis == "grp" else k + 1
        return (self.me + self.peers + away) % self.peers

    def to(self, j):
        return remote(self.out_ref(j), self.in_ref(self.me), self.send(j), self.recv(self.me), {self.axis: j})

    def own(self):
        return pltpu.make_async_copy(self.out_ref(self.me), self.in_ref(self.me), self.recv(self.me))

    def start(self, begin=0, end=None):
        loop((self.peers - 1 if end is None else end) - begin, lambda k: self.to(self.peer(k + begin)).start())

    def arrive(self, j):
        remote(self.out_ref(j), self.in_ref(j), self.send(j), self.recv(j), {self.axis: j}).wait_recv()

    def finish(self):
        self.own().wait()
        loop(self.peers - 1, lambda k: self.arrive(self.peer(k)))

    def drain(self):
        loop(self.peers - 1, lambda k: self.to(self.peer(k)).wait_send())


def kernel(
    groups,
    members,
    q_lat,
    q_rope,
    new_latent,
    prefix_shard,
    store_order,
    prefix_of_group,
    private_store,
    request_source,
    private_len,
    out,
    q_out,
    q_in,
    one_out,
    one_in,
    two_out,
    two_in,
    pref,
    scores,
    weighted,
    top,
    total,
    pages_in,
    pages_out0,
    pages_out1,
    keys0,
    keys1,
    part_out0,
    part_out1,
    part_in0,
    part_in1,
    slots,
    one_send,
    one_recv,
    two_send,
    two_recv,
    ring_send,
    ring_recv,
    pages_send,
    pages_recv,
    keys_send,
    keys_recv,
    q_send,
    q_recv,
    part_send,
    part_recv,
):
    me, mine = lax.axis_index("rep"), lax.axis_index("grp")
    half = members // 2
    z, y = mine // 2, mine % 2
    latent, rope = q_lat.shape[1], q_rope.shape[1]
    lanes = latent // 4
    requests = request_source.shape[0]
    owned = requests // members
    capacity, depth = private_store.shape[1:3]
    own_rows = q_lat.shape[0] // members
    block = own_rows // owned
    shard = prefix_shard.shape[0]

    def rows_of(j):
        return pl.ds(pl.multiple_of((j // 4) * 16, 16), 16)

    def columns_of(j):
        return pl.ds(pl.multiple_of((j % 4) * lanes, lanes), lanes)

    def cut(j):
        one_out[j, pl.ds(0, 16)] = prefix_shard[rows_of(j), columns_of(j)]

    def cut_rope(j):
        sides = [prefix_shard[pl.ds(pl.multiple_of((j % 4) * 32 + 16 * side, 16), 16), pl.ds(latent, rope)] for side in (0, 1)]
        one_out[j, pl.ds(16, 16)] = jnp.concatenate(sides, axis=1)

    loop(groups, cut)
    loop(groups, cut_rope)

    def query_rows(j):
        return pl.ds(pl.multiple_of(j * own_rows, own_rows), own_rows)

    def put_query(j):
        q_out[j, :, pl.ds(0, latent)] = q_lat[query_rows(j)]
        q_out[j, :, pl.ds(latent, lanes)] = jnp.concatenate(
            [q_rope[query_rows(j)], jnp.zeros((own_rows, lanes - rope), jnp.bfloat16)], axis=1
        )

    loop(members, put_query)
    greet(groups, members)
    one = Exchange("rep", groups, lambda j: one_out.at[j], lambda j: one_in.at[j], lambda j: one_send.at[j], lambda j: one_recv.at[j])
    two = Exchange("rep", groups, lambda j: two_out.at[j], lambda j: two_in.at[j], lambda j: two_send.at[j], lambda j: two_recv.at[j])
    pages = Exchange("rep", groups, lambda j: private_store.at[j], lambda j: pages_in.at[j], lambda j: pages_send.at[j], lambda j: pages_recv.at[j])
    queries = Exchange("grp", members, lambda j: q_out.at[j], lambda j: q_in.at[j], lambda j: q_send.at[j], lambda j: q_recv.at[j])

    def exchange_of(a, outs, ins, send, recv):
        return Exchange("grp", members, lambda j: outs[a].at[j], lambda j: ins[a].at[j], lambda j: send.at[a, j], lambda j: recv.at[a, j])

    def key_exchange(a):
        return exchange_of(a, (pages_out0, pages_out1), (keys0, keys1), keys_send, keys_recv)

    def part_exchange(a):
        return exchange_of(a, (part_out0, part_out1), (part_in0, part_in1), part_send, part_recv)

    one.start()
    one.own().start()

    @pl.when(me % 2 == 1)
    def _():
        queries.start()

    @pl.when(me % 2 == 0)
    def _():
        pages.start(0, EARLY)

    pages.own().start()
    queries.own().start()
    one.finish()

    def choose(j):
        two_out[j] = one_in[store_order[prefix_of_group[j]]]

    loop(groups, choose)
    two.start()
    two.own().start()

    @pl.when(me % 2 == 0)
    def _():
        pages.start(EARLY, groups - 1)

        queries.start()

    def find_slot(i):
        source = request_source[i]

        def count(j, rank):
            return rank + jnp.where((request_source[j] == source) & (j < i), 1, 0)

        slots[i] = jnp.minimum(lax.fori_loop(0, requests, count, jnp.int32(0)), capacity - 1)

    loop(requests, find_slot)
    two.finish()

    def place(j):
        pref[mine, rows_of(j), columns_of(j)] = two_in[j, pl.ds(0, 16)]

    def place_rope(j):
        pref[mine, pl.ds(shard, 16), columns_of(j)] = two_in[j, pl.ds(16, 16)]

    loop(groups, place)
    loop(4, place_rope)

    across = {"grp": z * 2 + 1 - y}
    up, down = {"grp": ((z + 1) % half) * 2 + y}, {"grp": ((z + half - 1) % half) * 2 + y}

    def shard_of(dz, column):
        return ((z + dz + half) % half) * 2 + column

    def ring(c, way, where):
        return remote(pref.at[c], pref.at[c], ring_send.at[way, c], ring_recv.at[c], where)

    def arrived(c):
        ring(c, 0, up).wait_recv()

    sends = []

    def send_on(c, way, where):
        ring(c, way, where).start()
        sends.append((c, way, where))

    other = shard_of(0, 1 - y)
    send_on(mine, 0, up)
    send_on(mine, 1, down)
    send_on(mine, 2, across)
    def attend(a, earlier):
        rows = members * block
        q = q_in[:, pl.ds(a * block, block), :].reshape(rows, latent + lanes)[:, : latent + rope]
        k_lat = (keys0[:, :, pl.ds(0, latent)], keys1[...])[a].reshape(members * depth, latent)
        k_rope = keys0[:, :, pl.ds(latent, lanes)].reshape(members * depth, lanes)[:, rope * a : rope * (a + 1)]
        s = (contract_last(q[:, :latent], k_lat) + contract_last(q[:, latent:], k_rope)) * score_scale
        usable = lax.broadcasted_iota(jnp.int32, s.shape, 1) < private_len[mine * owned + a]
        s = jnp.where(usable, s, very_negative)
        fresh = new_latent[mine * owned + a].astype(jnp.float32)
        q32 = q.astype(jnp.float32)
        step = (lax.broadcasted_iota(jnp.int32, (rows, 1), 0) % block) // (block // 2)
        new_s = []
        for u in range(2):
            s_u = jnp.sum(q32 * fresh[u : u + 1], axis=1, keepdims=True) * score_scale
            new_s.append(jnp.where(step >= u, s_u, very_negative))
        m = jnp.maximum(jnp.max(s, axis=1, keepdims=True), jnp.maximum(new_s[0], new_s[1]))
        e = jnp.where(usable, jnp.exp(s - m), 0.0)
        length = jnp.sum(e, axis=1, keepdims=True)
        summed = jnp.dot(e.astype(jnp.bfloat16), k_lat, preferred_element_type=jnp.float32)
        for u in range(2):
            e_u = jnp.where(step >= u, jnp.exp(new_s[u] - m), 0.0)
            length = length + e_u
            summed = summed + e_u.astype(jnp.bfloat16).astype(jnp.float32) * fresh[u : u + 1, :latent]
        lse = m + jnp.log(length)
        high = lse.astype(jnp.bfloat16).astype(jnp.float32)
        middle = (lse - high).astype(jnp.bfloat16).astype(jnp.float32)
        low = lse - high - middle
        place = lax.broadcasted_iota(jnp.int32, (rows, lanes), 1)
        tail = jnp.where(place == 3 * a, high, jnp.where(place == 3 * a + 1, middle, jnp.where(place == 3 * a + 2, low, earlier)))
        (part_out0, part_out1)[a][:, :, pl.ds(0, latent)] = (summed / length).astype(jnp.bfloat16).reshape(members, block, latent)
        if a == 1:
            part_out1[:, :, pl.ds(latent, lanes)] = tail.astype(jnp.bfloat16).reshape(members, block, lanes)
        return tail

    def attend_both():
        tail = 0.0
        for a in range(2):
            key_exchange(a).finish()
            tail = attend(a, tail)
            part_exchange(a).start()
            part_exchange(a).own().start()

    tile = scores.shape[2]
    rows = q_lat.shape[0]
    top[...] = jnp.full_like(top, very_negative)
    total[...] = jnp.zeros_like(total)
    weighted[...] = jnp.zeros_like(weighted)

    def odd_pages(hop):
        if hop == ODD_PAGES:

            @pl.when(me % 2 == 1)
            def _():
                pages.start()

    def send_keys():
        pages.finish()

        def pick(j):
            first, second = [pages_in[request_source[2 * j + a], slots[2 * j + a]] for a in range(2)]
            pages_out0[j, :, pl.ds(0, latent)] = first[:, :latent]
            pages_out0[j, :, pl.ds(latent, lanes)] = jnp.concatenate([first[:, latent:], second[:, latent:]], axis=1)
            pages_out1[j] = second[:, :latent]

        loop(members, pick)
        for a in range(2):
            key_exchange(a).start()
            key_exchange(a).own().start()

    arrived(other)
    send_on(other, 0, up)
    send_on(other, 1, down)
    odd_pages(0)
    for hop in (1, 2, 3):
        for column in (0, 1):
            c = shard_of(-hop, column)
            arrived(c)
            if hop < 3 or column == 0:
                send_on(c, 0, up)
            c = shard_of(hop, column)
            arrived(c)
            if hop < 3 or column == 1:
                send_on(c, 1, down)
        odd_pages(hop)
        if hop == PICK_AFTER:
            send_keys()
    for column in (0, 1):
        arrived(shard_of(4, column))

    def score(i):
        k_lat = pref[pl.ds(2 * i, 2), pl.ds(0, shard)].reshape(tile, latent)
        packed = [pref[2 * i + n, pl.ds(shard, 16)] for n in range(2)]
        k_rope = jnp.concatenate([p[:, rope * b : rope * (b + 1)] for p in packed for b in range(shard // 16)], axis=0)
        q = q_out[...].reshape(rows, latent + lanes)
        s = (contract_last(q[:, :latent], k_lat) + contract_last(q[:, latent : latent + rope], k_rope)) * score_scale
        scores[i] = s
        top[...] = jnp.maximum(top[...], jnp.max(s, axis=1, keepdims=True))

    loop(half, score)

    def weigh(i):
        e = jnp.exp(scores[i] - top[...])
        total[...] += jnp.sum(e, axis=1, keepdims=True)
        k = pref[pl.ds(2 * i, 2), pl.ds(0, shard)].reshape(tile, latent)
        weighted[...] += jnp.dot(e.astype(jnp.bfloat16), k, preferred_element_type=jnp.float32)

    loop(half, weigh)
    queries.finish()
    attend_both()

    def merge(a, j):
        at = pl.ds(pl.multiple_of(j * own_rows + a * block, block), block)
        tail = part_in1[j, :, pl.ds(latent, lanes)].astype(jnp.float32)
        mine_of_tail = lax.broadcasted_iota(jnp.int32, tail.shape, 1) // 3 == a
        lse = jnp.sum(jnp.where(mine_of_tail, tail, 0.0), axis=1, keepdims=True)
        part = (part_in0[j], part_in1[j, :, pl.ds(0, latent)])[a].astype(jnp.float32)
        m = jnp.maximum(top[at], lse)
        scale, part_scale = jnp.exp(top[at] - m), jnp.exp(lse - m)
        share = 1.0 / (total[at] * scale + part_scale)
        out[at] = (weighted[at] * (scale * share) + part * (part_scale * share)).astype(jnp.bfloat16)

    for exchange in (one, two, pages, queries, key_exchange(0), key_exchange(1)):
        exchange.drain()
    for c, way, where in sends:
        ring(c, way, where).wait_send()
    part_exchange(0).finish()
    part_exchange(1).finish()

    def merge_two(i):
        for j in range(2):
            for a in range(2):
                merge(a, 2 * i + j)

    loop(members // 2, merge_two)
    for a in range(2):
        part_exchange(a).drain()


def attention(members, q_lat, q_rope, new_latent, prefix_shard, store_order, prefix_of_group, private_store, request_source, private_len):
    groups, capacity, depth, width = private_store.shape
    rows, latent = q_lat.shape
    rope = q_rope.shape[1]
    requests = new_latent.shape[0]
    owned = requests // members
    own = rows // members
    shard = prefix_shard.shape[0]
    lanes = latent // 4
    wide = latent + lanes
    bf16, f32 = jnp.bfloat16, jnp.float32
    vmem, smem, anywhere = [pl.BlockSpec(memory_space=m) for m in (pltpu.VMEM, pltpu.SMEM, pl.ANY)]
    dma = pltpu.SemaphoreType.DMA
    return pl.pallas_call(
        functools.partial(kernel, groups, members),
        out_shape=jax.ShapeDtypeStruct((rows, latent), bf16),
        in_specs=[vmem, vmem, vmem, vmem, smem, smem, anywhere, smem, smem],
        out_specs=vmem,
        scratch_shapes=[pltpu.VMEM((members, own, wide), bf16)] * 2
        + [pltpu.VMEM((groups, 32, lanes), bf16)] * 4
        + [
            pltpu.VMEM((members, shard + 16, latent), bf16),
            pltpu.VMEM((members // 2, rows, 2 * shard), f32),
            pltpu.VMEM((rows, latent), f32),
            pltpu.VMEM((rows, 1), f32),
            pltpu.VMEM((rows, 1), f32),
            pltpu.VMEM((groups, capacity, depth, width), bf16),
        ]
        + [pltpu.VMEM((members, depth, w), bf16) for w in (wide, latent)] * 2
        + [pltpu.VMEM((members, own // owned, w), bf16) for w in (latent, wide)] * 2
        + [
            pltpu.SMEM((requests,), jnp.int32),
        ]
        + [dma((groups,))] * 4
        + [dma((3, members)), dma((members,))]
        + [dma((groups,))] * 2
        + [dma((owned, members))] * 2
        + [dma((members,))] * 2
        + [dma((owned, members))] * 2,
        compiler_params=pltpu.CompilerParams(collective_id=0, has_side_effects=True, vmem_limit_bytes=24 * MIB),
        cost_estimate=pl.CostEstimate(flops=2_700_000_000, bytes_accessed=8_000_000, transcendentals=2_000_000),
    )(
        q_lat,
        q_rope,
        new_latent,
        prefix_shard,
        store_order,
        prefix_of_group,
        private_store,
        request_source,
        private_len,
    )


def shards(
    members,
    q_nope,
    q_rope,
    new_latent,
    w_uk,
    w_uv,
    prefix_store,
    store_order,
    prefix_of_group,
    private_store,
    request_source,
    private_len,
):
    requests, steps, heads = q_nope.shape[:3]
    rows = requests * steps * heads
    q_lat = jnp.einsum("rthn,hnc->rthc", q_nope, w_uk, preferred_element_type=jnp.float32).astype(jnp.bfloat16)
    q_lat, q_rope = q_lat.reshape(rows, -1), q_rope.reshape(rows, -1)
    attended = attention(
        members,
        q_lat,
        q_rope,
        new_latent,
        prefix_store[0],
        store_order,
        prefix_of_group,
        private_store[0],
        request_source[:, 0],
        private_len[0],
    )
    attended = attended.reshape(requests, steps, heads, -1)
    return jnp.einsum("rthc,hcv->rthv", attended, w_uv, preferred_element_type=jnp.float32).astype(jnp.bfloat16)


def solution(mesh):
    in_specs = (
        P("rep", None, "grp", None),
        P("rep", None, "grp", None),
        P("rep", None, None),
        P("grp", None, None),
        P("grp", None, None),
        P("rep", "grp", None),
        P(),
        P(),
        P("rep", None, None, "grp", None),
        P("rep", None),
        P("rep", None),
    )
    out_specs = P("rep", None, "grp", None)
    body = functools.partial(shards, mesh.shape["grp"])
    return jax.shard_map(body, mesh=mesh, in_specs=in_specs, out_specs=out_specs, check_vma=False)
```
